32 devices in a mesh: cfg: 2 (over y), tm: 4 (over z), space: 2 (over x), spin: 2 (over core).
Axes of the slice: x: 2, y: 2, z: 4, core: 2. Of those that a mesh axis runs over, the one named last changes fastest.
Arguments:
- eigenvectors: bfloat16 [8, 2, 3, 16, 2, 2, 128], P(('cfg', 'tm'), None, None, 'space'), parts along dimension 0, may hold values from -6 to 6
- gauge_links: bfloat16 [8, 3, 2, 3, 3, 16, 4], P(('cfg', 'tm'), None, None, None, None, 'space'), parts along dimension 0, may hold values from -2.4375 to 2.4375
- perambulators: bfloat16 [8, 512, 1024], P(('cfg', 'tm'), ('space', 'spin')), parts along dimension 0, may hold values from -0.1875 to 0.1875
- source_times: int32 [16], replicated, may hold values from 0 to 3
- insert_offsets: int32 [4], replicated, may hold values from 0 to 2
- derivative_dirs: int32 [3], replicated, may hold values from 0 to 2, each once
Outputs:
- elementals: float32 [8, 128, 3, 2, 128], P(('cfg', 'tm'), 'space', None, None, 'spin'), parts along dimension 0
- chain_products: bfloat16 [8, 512, 1024], P(('cfg', 'tm'), ('space', 'spin')), parts along dimension 0
- correlator: float32 [32, 2], P('cfg'), parts along dimension 0
The draws below stay inside these ranges and needn't reach their ends.
There are 2 independent parts, one for each index of `cfg`. The reference program is written for one: setup_inputs(seed, part) draws one part's arguments, and reference() takes and returns one part's arrays. A program takes and returns all parts, laid end to end along the dimension named above; an argument that names none is the same for every part. Nothing has to cross between parts.
Inputs may be any that keep to these rules, and one draw needn't show every extreme that they name: `derivative_dirs`: each of 0, 1, 2 appears once.
All inputs are finite; a program needn't handle non-finite values.
Results may differ from the reference program's by a relative error of at most 0.012.
Values may be sent and summed in bfloat16 or wider, within the bound.
No kernel may reach another device: no remote copies, remote signals or barrier semaphores. Data moves between devices by JAX's collectives and lax.ppermute only.
A program may use at most 64 MiB of HBM per device.

```python
import math
import jax
import jax.numpy as jnp
import numpy as np
from jax import lax

MODES = 128
ORDER = 512
SIDE = 2
DEPTH = 16
TIMES = 4
SOURCES = 16
INSERTS = 4


def plant(values, key, low, largest):
    extent = values.shape
    index_at = [jax.random.randint(jax.random.fold_in(key, axis), (), 0, extent[axis]) for axis in range(len(extent))]
    values = values.at[tuple(index_at)].set(low)
    longest = extent.index(max(extent))
    index_at[longest] = (index_at[longest] + 1) % extent[longest]
    return values.at[tuple(index_at)].set(largest)


def level_of(key, dims, pieces, smallest, top_value):
    factor_of = 1.0
    for axis_at, blocks in pieces:
        heights = jax.random.uniform(jax.random.fold_in(jax.random.fold_in(key, 6), axis_at), (blocks,), jnp.float32, smallest / len(pieces), top_value / len(pieces))
        factor_of = factor_of * jnp.repeat(jnp.exp(heights), dims[axis_at] // blocks).reshape((-1,) + (1,) * (len(dims) - 1 - axis_at))
    return factor_of


def bell_draw(own_key, extent, deviation, limit, shards=(), kind=jnp.bfloat16):
    gain = level_of(own_key, extent, shards, -0.22, 0.18) if shards else 1.0
    entries = jax.random.normal(own_key, extent, jnp.float32) * deviation * gain
    return jnp.minimum(jnp.maximum(entries, -limit), limit).astype(kind)


def setup_inputs(seed: int = 0, part: int = 0) -> dict:
    keys = jax.random.split(jax.random.key(seed), 7)
    part_keys = jax.random.split(jax.random.fold_in(keys[6], part), 7)
    eigenvectors = bell_draw(part_keys[0], (TIMES, 2, 3, DEPTH, SIDE, SIDE, MODES), 1.0, 6.0, ((0, 4), (3, 2)))
    gauge_links = bell_draw(part_keys[1], (TIMES, 3, 2, 3, 3, DEPTH, SIDE * SIDE), 0.408, 2.4375, ((0, 4), (5, 2)))
    perambulators = bell_draw(part_keys[2], (TIMES, ORDER, 2 * ORDER), (2 * ORDER) ** -0.5, 0.1875, ((0, 4), (1, 4)))
    source_times = plant(jax.random.randint(keys[3], (SOURCES,), 0, TIMES), jax.random.fold_in(keys[3], 1), 0, TIMES - 1).astype(jnp.int32)
    insert_offsets = plant(jax.random.randint(keys[4], (INSERTS,), 0, 3), jax.random.fold_in(keys[4], 1), 0, 2).astype(jnp.int32)
    derivative_dirs = jax.random.permutation(keys[5], 3).astype(jnp.int32)
    return dict(eigenvectors=eigenvectors, gauge_links=gauge_links, perambulators=perambulators, source_times=source_times, insert_offsets=insert_offsets, derivative_dirs=derivative_dirs)


def gamma_tables():
    sigma_real = np.zeros((3, 2, 2), np.float32)
    sigma_imag = np.zeros((3, 2, 2), np.float32)
    sigma_real[0] = [[0.0, 1.0], [1.0, 0.0]]
    sigma_imag[1] = [[0.0, -1.0], [1.0, 0.0]]
    sigma_real[2] = [[1.0, 0.0], [0.0, -1.0]]
    gamma_real = np.zeros((3, 4, 4), np.float32)
    gamma_imag = np.zeros((3, 4, 4), np.float32)
    gamma_real[:, 0:2, 2:4] = sigma_imag
    gamma_imag[:, 0:2, 2:4] = -sigma_real
    gamma_real[:, 2:4, 0:2] = -sigma_imag
    gamma_imag[:, 2:4, 0:2] = sigma_real
    return (gamma_real, gamma_imag)

def color_product(matrix, vectors):
    return lax.optimization_barrier(jnp.sum(matrix[:, :, :, :, :, None] * vectors[None], axis=1))

def times_links(link_field, vectors):
    real_part = color_product(link_field[0], vectors[0]) - color_product(link_field[1], vectors[1])
    imag_part = color_product(link_field[0], vectors[1]) + color_product(link_field[1], vectors[0])
    return jnp.stack([real_part, imag_part])

def times_adjoint(link_field, vectors):
    swapped = jnp.swapaxes(link_field, 1, 2)
    real_part = color_product(swapped[0], vectors[0]) + color_product(swapped[1], vectors[1])
    imag_part = color_product(swapped[0], vectors[1]) - color_product(swapped[1], vectors[0])
    return jnp.stack([real_part, imag_part])

def block_matrix(real_part, imag_part):
    upper_half = jnp.concatenate([real_part, imag_part], axis=1)
    lower_half = jnp.concatenate([-imag_part, real_part], axis=1)
    return jnp.concatenate([upper_half, lower_half], axis=0)

def row_block(matrix_rows):
    matrix_order = matrix_rows.shape[1] // 2
    return block_matrix(matrix_rows[:, :matrix_order], matrix_rows[:, matrix_order:])

def operator_matrix(elementals_wide, derivative_dirs):
    gamma_real, gamma_imag = gamma_tables()
    select = (derivative_dirs[:, None] == jnp.arange(3, dtype=jnp.int32)[None, :]).astype(jnp.float32)
    mixed_real = jnp.einsum('km,kpq->mpq', select, jnp.asarray(gamma_real), precision=lax.Precision.HIGHEST)
    mixed_imag = jnp.einsum('km,kpq->mpq', select, jnp.asarray(gamma_imag), precision=lax.Precision.HIGHEST)
    elem_real = elementals_wide[:, :, 0, :]
    elem_imag = elementals_wide[:, :, 1, :]
    pattern = 'mpq,amb->paqb'
    real_part = jnp.einsum(pattern, mixed_real, elem_real, precision=lax.Precision.HIGHEST) - jnp.einsum(pattern, mixed_imag, elem_imag, precision=lax.Precision.HIGHEST)
    imag_part = jnp.einsum(pattern, mixed_real, elem_imag, precision=lax.Precision.HIGHEST) + jnp.einsum(pattern, mixed_imag, elem_real, precision=lax.Precision.HIGHEST)
    matrix_order = 4 * elementals_wide.shape[0]
    real_part = real_part.reshape((matrix_order, matrix_order)).astype(jnp.bfloat16)
    imag_part = imag_part.reshape((matrix_order, matrix_order)).astype(jnp.bfloat16)
    return block_matrix(real_part, imag_part)

def trace_pair(product):
    matrix_order = product.shape[1] // 2
    return jnp.stack([jnp.trace(product[:, :matrix_order]), jnp.trace(product[:, matrix_order:])])

def correlate(traces, source_times, insert_offsets):
    slot_count = traces.shape[0]
    counts = lax.optimization_barrier(jnp.sum((insert_offsets[:, None] == jnp.arange(3, dtype=jnp.int32)[None, :]).astype(jnp.float32), axis=0))
    weighted = lax.optimization_barrier(jnp.sum(traces * counts[None, :, None], axis=1))
    picker = (source_times[:, None] == jnp.arange(slot_count, dtype=jnp.int32)[None, :]).astype(jnp.float32)
    return jnp.dot(picker, weighted, precision=lax.Precision.HIGHEST)

def slice_elementals(vectors, link_block, norm_scale):
    depth_cells, side_cells = (vectors.shape[2], vectors.shape[3])
    mode_count = vectors.shape[5]
    vectors_wide = vectors.astype(jnp.float32)
    columns = []
    for direction in range(3):
        spatial_axis = 4 - direction
        link_field = link_block[direction].reshape((2, 3, 3, depth_cells, side_cells, side_cells)).astype(jnp.float32)
        forward_field = jnp.roll(vectors_wide, -1, axis=spatial_axis)
        adjoint = times_adjoint(link_field, vectors_wide).astype(jnp.bfloat16)
        behind = lax.optimization_barrier(jnp.roll(adjoint, 1, axis=spatial_axis)).astype(jnp.float32)
        derived = (times_links(link_field, forward_field) - behind).astype(jnp.bfloat16)
        columns.append(derived.reshape((-1, mode_count)))
        columns.append(jnp.concatenate([derived[1], -derived[0]], axis=0).reshape((-1, mode_count)))
    stacked = jnp.stack(columns, axis=1).reshape((columns[0].shape[0], -1))
    flat_vectors = vectors.reshape((-1, mode_count))
    partial_sum = lax.dot_general(flat_vectors, stacked, (((0,), (0,)), ((), ())), preferred_element_type=jnp.float32)
    return (partial_sum * norm_scale).reshape((mode_count, 3, 2, mode_count))

def reference(eigenvectors, gauge_links, perambulators, source_times, insert_offsets, derivative_dirs):
    norm_scale = 1.0 / math.sqrt(24.0 * DEPTH * SIDE * SIDE)

    def first_section(inputs):
        vectors, link_block, peram_rows = inputs
        elementals = slice_elementals(vectors, link_block, norm_scale)
        rounded = lax.optimization_barrier(elementals.astype(jnp.bfloat16)).astype(jnp.float32)
        operator = operator_matrix(rounded, derivative_dirs)
        first_product = jnp.dot(peram_rows, operator, preferred_element_type=jnp.float32) * (1.0 / math.sqrt(ORDER))
        return (elementals, first_product.astype(jnp.bfloat16), trace_pair(first_product))
    elementals, first_rounded, first_traces = lax.map(first_section, (eigenvectors, gauge_links, perambulators))

    def next_section(inputs):
        left_rows, right_rows = inputs
        product = jnp.dot(left_rows, row_block(right_rows), preferred_element_type=jnp.float32)
        return (product.astype(jnp.bfloat16), product, trace_pair(product))
    second_rounded, second_product, second_traces = lax.map(next_section, (jnp.roll(first_rounded, -1, axis=0), first_rounded))
    third_rounded, third_product, third_traces = lax.map(next_section, (jnp.roll(second_rounded, -1, axis=0), first_rounded))
    chain_products = (third_product * math.sqrt(ORDER)).astype(jnp.bfloat16)
    traces = jnp.stack([first_traces, second_traces, third_traces], axis=1)
    correlator = correlate(traces, source_times, insert_offsets)
    return (elementals, chain_products, correlator)
```

```python
import functools
import math

import jax
import jax.numpy as jnp
from jax import lax
from jax.experimental import pallas as pl
from jax.experimental.pallas import tpu as pltpu

from jax.sharding import PartitionSpec as P

F32 = jnp.float32
BF16 = jnp.bfloat16


def from_offset(block, axis, distance):
    count = lax.axis_size(axis)
    return lax.ppermute(block, axis, [((i + distance) % count, i) for i in range(count)])


def from_diagonal(block, slot_step, space_step):
    slots, spaces = lax.axis_size("tm"), lax.axis_size("space")
    route = []
    for slot in range(slots):
        for place in range(spaces):
            source = ((slot + slot_step) % slots) * spaces + (place + space_step) % spaces
            route.append((source, slot * spaces + place))
    return lax.ppermute(block, ("tm", "space"), route)


def vmem_call(kernel, out_shape, scratch, flops, smem=()):
    def call(*operands):
        specs = [
            pl.BlockSpec(memory_space=pltpu.SMEM if i in smem else pltpu.VMEM)
            for i in range(len(operands))
        ]
        outs = jax.tree.map(lambda _: pl.BlockSpec(memory_space=pltpu.VMEM), out_shape)
        return pl.pallas_call(
            kernel,
            out_shape=out_shape,
            in_specs=specs,
            out_specs=outs,
            scratch_shapes=scratch,
            compiler_params=pltpu.CompilerParams(vmem_limit_bytes=40 * 1024 * 1024),
            cost_estimate=pl.CostEstimate(
                flops=flops, bytes_accessed=1 << 20, transcendentals=0
            ),
        )(*operands)

    return call


def moved(field, distance):
    rows = field.shape[0]
    return pltpu.roll(field, distance % rows, 0) if distance % rows else field


def ahead_of(field, stride, side):
    row = lax.broadcasted_iota(jnp.int32, field.shape, 0)
    last = (row // stride) % side == side - 1
    return jnp.where(last, moved(field, (side - 1) * stride), moved(field, -stride))


def behind_of(field, stride, side):
    row = lax.broadcasted_iota(jnp.int32, field.shape, 0)
    start = (row // stride) % side == 0
    return jnp.where(start, moved(field, (1 - side) * stride), moved(field, stride))


def elementals_kernel(cells, side, scale, slabs, dirs_ref, *refs):
    slab_refs, (elem_ref, oper_ref, rhs_ref, pick_ref) = refs[:-4], refs[-4:]
    slot_count = len(slab_refs) // slabs
    modes = elem_ref.shape[-1]
    for slot in range(slot_count):
        mine = slab_refs[slot * slabs : (slot + 1) * slabs]
        fields = [
            jnp.concatenate([ref[k * cells : (k + 1) * cells, :] for ref in mine], axis=0)
            for k in range(6)
        ]
        vectors = jnp.concatenate(fields, axis=0)
        links = jnp.concatenate([ref[6 * cells : 7 * cells, :] for ref in mine], axis=0).astype(F32)
        sites = slabs * cells
        wide = [field.astype(F32) for field in fields]
        for direction in range(3):
            stride = side**direction
            across = side if direction < 2 else sites // stride
            forward = [ahead_of(field, stride, across) for field in wide]
            terms = [[None] * 3 for _ in range(4)]
            for colour in range(3):
                for other in range(3):
                    at = direction * 18 + colour * 3 + other
                    link_real = links[:, at : at + 1]
                    link_imag = links[:, at + 9 : at + 10]
                    ahead_real, ahead_imag = forward[other], forward[3 + other]
                    here_real, here_imag = wide[colour], wide[3 + colour]
                    for kind, to, term in (
                        (0, colour, link_real * ahead_real - link_imag * ahead_imag),
                        (1, colour, link_real * ahead_imag + link_imag * ahead_real),
                        (2, other, link_real * here_real + link_imag * here_imag),
                        (3, other, link_real * here_imag - link_imag * here_real),
                    ):
                        held = terms[kind][to]
                        terms[kind][to] = term if held is None else held + term
            left, right = 2 * direction * modes, (2 * direction + 1) * modes
            for colour in range(3):
                parts = []
                for kind in range(2):
                    adjoint = terms[2 + kind][colour].astype(BF16).astype(F32)
                    parts.append(terms[kind][colour] - behind_of(adjoint, stride, across))
                real_part, imag_part = parts[0], parts[1]
                low, high = colour * sites, (3 + colour) * sites
                rhs_ref[low : low + sites, left : left + modes] = real_part.astype(BF16)
                rhs_ref[high : high + sites, left : left + modes] = imag_part.astype(BF16)
                rhs_ref[low : low + sites, right : right + modes] = imag_part.astype(BF16)
                rhs_ref[high : high + sites, right : right + modes] = (-real_part).astype(BF16)
        product = lax.dot_general(
            vectors, rhs_ref[...], (((0,), (0,)), ((), ())), preferred_element_type=F32
        )
        for direction in range(3):
            left = 2 * direction * modes
            real_part = product[:, left : left + modes] * scale
            imag_part = product[:, left + modes : left + 2 * modes] * scale
            if slot == 0:
                elem_ref[direction, 0] = real_part
                elem_ref[direction, 1] = imag_part
            pick_ref[direction, 0] = real_part.astype(BF16).astype(F32)
            pick_ref[direction, 1] = imag_part.astype(BF16).astype(F32)
        zero_real, zero_imag = pick_ref[dirs_ref[0], 0], pick_ref[dirs_ref[0], 1]
        one_real, one_imag = pick_ref[dirs_ref[1], 0], pick_ref[dirs_ref[1], 1]
        two_real, two_imag = pick_ref[dirs_ref[2], 0], pick_ref[dirs_ref[2], 1]
        sum_real = [[two_real, zero_real + one_imag], [zero_real - one_imag, -two_real]]
        sum_imag = [[two_imag, zero_imag - one_real], [zero_imag + one_real, -two_imag]]
        for p in range(2):
            for q in range(2):
                top, bottom = p * modes, (2 + p) * modes
                left, right = q * modes, (2 + q) * modes
                real_part = sum_real[p][q].astype(BF16)
                imag_part = sum_imag[p][q].astype(BF16)
                oper_ref[slot, top : top + modes, left : left + modes] = -imag_part
                oper_ref[slot, top : top + modes, right : right + modes] = real_part
                oper_ref[slot, bottom : bottom + modes, left : left + modes] = -real_part
                oper_ref[slot, bottom : bottom + modes, right : right + modes] = -imag_part


def times_operator(rows, operator):
    half = rows.shape[1] // 4
    upper = jnp.concatenate([rows[:, half : 2 * half], rows[:, 3 * half :]], axis=1)
    lower = jnp.concatenate([rows[:, :half], rows[:, 2 * half : 3 * half]], axis=1)
    both = jnp.dot(
        jnp.concatenate([upper, lower], axis=0), operator, preferred_element_type=F32
    )
    scale = 1.0 / math.sqrt(2.0 * half)
    count = rows.shape[0]
    above = both[:count] * scale
    below = both[count:] * (-scale)
    return jnp.concatenate([above[:, :half], below[:, :half], above[:, half:], below[:, half:]], 1)


def times_rows(left, right):
    order = left.shape[1] // 2
    count = left.shape[0]
    both = jnp.dot(
        jnp.concatenate([left[:, :order], left[:, order:]], axis=0),
        right,
        preferred_element_type=F32,
    )
    real_part = both[:count, :order] - both[count:, order:]
    imag_part = both[:count, order:] + both[count:, :order]
    return real_part, imag_part


def diagonal_sum(part, first_row):
    row = lax.broadcasted_iota(jnp.int32, part.shape, 0) + first_row
    column = lax.broadcasted_iota(jnp.int32, part.shape, 1)
    kept = jnp.where(row == column, part, 0.0)
    return jnp.sum(jnp.sum(kept, axis=0, keepdims=True), axis=1, keepdims=True)


def at_lanes(shape, values):
    lane = lax.broadcasted_iota(jnp.int32, shape, 1)
    total = jnp.zeros(shape, F32)
    for at, value in values:
        total = total + jnp.where(lane == at, value, 0.0)
    return total


def own_block(spaces, spins, space_step, spin_step):
    place = lax.rem(lax.axis_index("space") + space_step, spaces)
    spin = lax.rem(lax.axis_index("spin") + spin_step, spins)
    return place * spins + spin


def second_kernel(spaces, spins, oper_ref, next_ref, *refs):
    block_refs, (first_ref, second_ref, trace_ref) = refs[:-3], refs[-3:]
    count = next_ref.shape[0]
    order = next_ref.shape[1] // 2
    first_row = own_block(spaces, spins, 0, 0) * count
    for at, block_ref in enumerate(block_refs):
        product = times_operator(block_ref[...], oper_ref[0])
        start = pl.multiple_of(own_block(spaces, spins, at // spins, at % spins) * count, count)
        first_ref[pl.ds(start, count), :] = product.astype(BF16)
        if at == 0:
            first_real = diagonal_sum(product[:, :order], first_row)
            first_imag = diagonal_sum(product[:, order:], first_row)
    left = times_operator(next_ref[...], oper_ref[1]).astype(BF16)
    real_part, imag_part = times_rows(left, first_ref[...])
    second_ref[:, :order] = real_part.astype(BF16)
    second_ref[:, order:] = imag_part.astype(BF16)
    trace_ref[...] = at_lanes(
        trace_ref.shape,
        [
            (0, first_real),
            (1, first_imag),
            (2, diagonal_sum(real_part, first_row)),
            (3, diagonal_sum(imag_part, first_row)),
        ],
    )


def third_kernel(spaces, spins, second_ref, first_ref, early_ref, chain_ref, trace_ref):
    count = second_ref.shape[0]
    order = second_ref.shape[1] // 2
    first_row = own_block(spaces, spins, 0, 0) * count
    real_part, imag_part = times_rows(second_ref[...], first_ref[...])
    scale = math.sqrt(order)
    chain_ref[:, :order] = (real_part * scale).astype(BF16)
    chain_ref[:, order:] = (imag_part * scale).astype(BF16)
    late = at_lanes(
        early_ref.shape,
        [(4, diagonal_sum(real_part, first_row)), (5, diagonal_sum(imag_part, first_row))],
    )
    row = lax.broadcasted_iota(jnp.int32, trace_ref.shape, 0)
    values = jnp.broadcast_to((early_ref[...] + late)[0:1], trace_ref.shape)
    trace_ref[...] = jnp.where(row == lax.axis_index("tm"), values, 0.0)


def correlator_kernel(offsets_ref, times_ref, *refs):
    part_refs, out_ref = refs[:-1], refs[-1]
    traces = part_refs[0][...]
    for part_ref in part_refs[1:]:
        traces = traces + part_ref[...]
    lane = lax.broadcasted_iota(jnp.int32, (1, traces.shape[1]), 1)
    counts = jnp.zeros((1, traces.shape[1]), F32)
    for j in range(offsets_ref.shape[0]):
        counts = counts + jnp.where(lane // 2 == offsets_ref[j], 1.0, 0.0)
    weighted = traces * counts
    row = lax.broadcasted_iota(jnp.int32, (traces.shape[0], times_ref.shape[1]), 0)
    chosen = row == times_ref[...]
    for part in range(2):
        keep = (lane % 2 == part) & (lane < 6)
        column = jnp.sum(jnp.where(keep, weighted, 0.0), axis=1, keepdims=True)
        out_ref[part : part + 1, :] = jnp.sum(
            jnp.where(chosen, column, 0.0), axis=0, keepdims=True
        )


def on_device(
    eigenvectors, gauge_links, perambulators, source_times, insert_offsets, derivative_dirs
):
    spaces, spins, slots = lax.axis_size("space"), lax.axis_size("spin"), lax.axis_size("tm")
    planes, side, modes = eigenvectors.shape[3], eigenvectors.shape[4], eigenvectors.shape[6]
    cells = planes * side * side
    own_rows = perambulators[0]
    count, width = own_rows.shape
    order = width // 2

    vectors = eigenvectors.reshape((6 * cells, modes))
    links = gauge_links.reshape((54, cells)).T
    links = jnp.pad(links, ((0, 0), (0, modes - 54)))
    pack = jnp.concatenate([vectors, links], axis=0)

    slabs = [pack] + [from_offset(pack, "space", step) for step in range(1, spaces)]
    slabs.append(from_offset(pack, "tm", 1))
    slabs += [from_diagonal(pack, 1, step) for step in range(1, spaces)]

    next_rows = from_offset(own_rows, "tm", 1)
    blocks = []
    for space_step in range(spaces):
        block = own_rows if space_step == 0 else from_offset(own_rows, "space", space_step)
        blocks.append(block)
        for spin_step in range(1, spins):
            blocks.append(from_offset(block, "spin", spin_step))

    norm_scale = 1.0 / math.sqrt(6.0 * 4.0 * planes * spaces * side * side)
    elements, operators = vmem_call(
        functools.partial(elementals_kernel, cells, side, norm_scale, spaces),
        (
            jax.ShapeDtypeStruct((3, 2, modes, modes), F32),
            jax.ShapeDtypeStruct((2, 4 * modes, 4 * modes), BF16),
        ),
        [
            pltpu.VMEM((6 * cells * spaces, 6 * modes), BF16),
            pltpu.VMEM((3, 2, modes, modes), F32),
        ],
        10**8,
        smem=(0,),
    )(derivative_dirs, *slabs)

    first, second, early = vmem_call(
        functools.partial(second_kernel, spaces, spins),
        (
            jax.ShapeDtypeStruct((order, width), BF16),
            jax.ShapeDtypeStruct((count, width), BF16),
            jax.ShapeDtypeStruct((8, 128), F32),
        ),
        [],
        10**9,
    )(operators, next_rows, *blocks)

    next_second = from_offset(second, "tm", 1)

    rows, columns = modes // spaces, modes // spins
    share = lax.dynamic_slice(
        elements,
        (0, 0, lax.axis_index("space") * rows, lax.axis_index("spin") * columns),
        (3, 2, rows, columns),
    )
    elementals = jnp.transpose(share, (2, 0, 1, 3))

    chain, traces = vmem_call(
        functools.partial(third_kernel, spaces, spins),
        (
            jax.ShapeDtypeStruct((count, width), BF16),
            jax.ShapeDtypeStruct((-(-slots // 8) * 8, 128), F32),
        ),
        [],
        3 * 10**8,
    )(next_second, first, early)

    group = spaces * spins
    parts = [traces] + [from_offset(traces, ("space", "spin"), step) for step in range(1, group)]
    traces = functools.reduce(lambda a, b: a + b, parts)
    if slots & (slots - 1):
        parts = [lax.psum(traces, "tm")]
    else:
        step = 1
        while step < slots:
            other = lax.ppermute(traces, "tm", [(i ^ step, i) for i in range(slots)])
            parts = [traces, other]
            traces = traces + other
            step *= 2
    correlator = vmem_call(
        correlator_kernel,
        jax.ShapeDtypeStruct((2, source_times.shape[0]), F32),
        [],
        10**5,
        smem=(0,),
    )(insert_offsets, source_times[None, :], *parts)
    return (elementals[None], chain[None], correlator.T)


def solution(mesh):
    in_specs = (
        P(("cfg", "tm"), None, None, "space", None, None, None),
        P(("cfg", "tm"), None, None, None, None, "space", None),
        P(("cfg", "tm"), ("space", "spin"), None),
        P(),
        P(),
        P(),
    )
    out_specs = (
        P(("cfg", "tm"), "space", None, None, "spin"),
        P(("cfg", "tm"), ("space", "spin"), None),
        P("cfg", None),
    )
    return jax.shard_map(
        on_device, mesh=mesh, in_specs=in_specs, out_specs=out_specs, check_vma=False
    )
```

```python
import functools
import math

import jax
import jax.numpy as jnp
from jax import lax
from jax.experimental import pallas as pl
from jax.experimental.pallas import tpu as pltpu

from jax.sharding import PartitionSpec as P

F32 = jnp.float32
BF16 = jnp.bfloat16
PIECES = 2


def from_offset(block, axis, distance):
    count = lax.axis_size(axis)
    return lax.ppermute(block, axis, [((i + distance) % count, i) for i in range(count)])


def vmem_call(kernel, out_shape, scratch, flops, smem=()):
    def call(*operands):
        specs = [
            pl.BlockSpec(memory_space=pltpu.SMEM if i in smem else pltpu.VMEM)
            for i in range(len(operands))
        ]
        outs = jax.tree.map(lambda _: pl.BlockSpec(memory_space=pltpu.VMEM), out_shape)
        return pl.pallas_call(
            kernel,
            out_shape=out_shape,
            in_specs=specs,
            out_specs=outs,
            scratch_shapes=scratch,
            compiler_params=pltpu.CompilerParams(vmem_limit_bytes=16 * 1024 * 1024),
            cost_estimate=pl.CostEstimate(
                flops=flops, bytes_accessed=1 << 20, transcendentals=0
            ),
        )(*operands)

    return call


def moved(field, distance):
    rows = field.shape[0]
    return pltpu.roll(field, distance % rows, 0) if distance % rows else field


def ahead_of(field, stride, side):
    row = lax.broadcasted_iota(jnp.int32, field.shape, 0)
    last = (row // stride) % side == side - 1
    return jnp.where(last, moved(field, (side - 1) * stride), moved(field, -stride))


def behind_of(field, stride, side):
    row = lax.broadcasted_iota(jnp.int32, field.shape, 0)
    start = (row // stride) % side == 0
    return jnp.where(start, moved(field, (1 - side) * stride), moved(field, stride))


def elementals_kernel(cells, side, scale, slabs, spins, dirs_ref, rows_ref, *refs):
    slab_refs, out_refs = refs[:slabs], refs[slabs:]
    elem_ref, oper_ref, first_ref, trace_ref, rhs_ref, pick_ref = out_refs
    modes = pick_ref.shape[-1]
    sites = slabs * cells
    fields = [
        jnp.concatenate([ref[k * cells : (k + 1) * cells, :] for ref in slab_refs], axis=0)
        for k in range(6)
    ]
    vectors = jnp.concatenate(fields, axis=0)
    links = jnp.concatenate([ref[6 * cells : 7 * cells, :] for ref in slab_refs], axis=0)
    links = links.astype(F32)
    wide = [field.astype(F32) for field in fields]
    for direction in range(3):
        stride = side**direction
        across = side if direction < 2 else sites // stride
        forward = [ahead_of(field, stride, across) for field in wide]
        terms = [[None] * 3 for _ in range(4)]
        for colour in range(3):
            for other in range(3):
                at = direction * 18 + colour * 3 + other
                link_real = links[:, at : at + 1]
                link_imag = links[:, at + 9 : at + 10]
                ahead_real, ahead_imag = forward[other], forward[3 + other]
                here_real, here_imag = wide[colour], wide[3 + colour]
                for kind, to, term in (
                    (0, colour, link_real * ahead_real - link_imag * ahead_imag),
                    (1, colour, link_real * ahead_imag + link_imag * ahead_real),
                    (2, other, link_real * here_real + link_imag * here_imag),
                    (3, other, link_real * here_imag - link_imag * here_real),
                ):
                    held = terms[kind][to]
                    terms[kind][to] = term if held is None else held + term
        left, right = 2 * direction * modes, (2 * direction + 1) * modes
        for colour in range(3):
            parts = []
            for kind in range(2):
                adjoint = terms[2 + kind][colour].astype(BF16).astype(F32)
                parts.append(terms[kind][colour] - behind_of(adjoint, stride, across))
            real_part, imag_part = parts[0], parts[1]
            low, high = colour * sites, (3 + colour) * sites
            rhs_ref[low : low + sites, left : left + modes] = real_part.astype(BF16)
            rhs_ref[high : high + sites, left : left + modes] = imag_part.astype(BF16)
            rhs_ref[low : low + sites, right : right + modes] = imag_part.astype(BF16)
            rhs_ref[high : high + sites, right : right + modes] = (-real_part).astype(BF16)
    product = lax.dot_general(
        vectors, rhs_ref[...], (((0,), (0,)), ((), ())), preferred_element_type=F32
    )
    for direction in range(3):
        left = 2 * direction * modes
        real_part = product[:, left : left + modes] * scale
        imag_part = product[:, left + modes : left + 2 * modes] * scale
        elem_ref[direction, 0] = real_part
        elem_ref[direction, 1] = imag_part
        pick_ref[direction, 0] = real_part.astype(BF16).astype(F32)
        pick_ref[direction, 1] = imag_part.astype(BF16).astype(F32)
    zero_real, zero_imag = pick_ref[dirs_ref[0], 0], pick_ref[dirs_ref[0], 1]
    one_real, one_imag = pick_ref[dirs_ref[1], 0], pick_ref[dirs_ref[1], 1]
    two_real, two_imag = pick_ref[dirs_ref[2], 0], pick_ref[dirs_ref[2], 1]
    sum_real = [[two_real, zero_real + one_imag], [zero_real - one_imag, -two_real]]
    sum_imag = [[two_imag, zero_imag - one_real], [zero_imag + one_real, -two_imag]]
    for p in range(2):
        for q in range(2):
            top, bottom = p * modes, (2 + p) * modes
            left, right = q * modes, (2 + q) * modes
            real_part = sum_real[p][q].astype(BF16)
            imag_part = sum_imag[p][q].astype(BF16)
            oper_ref[top : top + modes, left : left + modes] = -imag_part
            oper_ref[top : top + modes, right : right + modes] = real_part
            oper_ref[bottom : bottom + modes, left : left + modes] = -real_part
            oper_ref[bottom : bottom + modes, right : right + modes] = -imag_part
    count, width = rows_ref.shape
    first_row = own_block(slabs, spins, 0, 0) * count
    product = times_operator(rows_ref[...], oper_ref[...])
    first_ref[...] = product.astype(BF16)
    trace_ref[...] = at_lanes(
        trace_ref.shape,
        [
            (0, diagonal_sum(product[:, : width // 2], first_row)),
            (1, diagonal_sum(product[:, width // 2 :], first_row)),
        ],
    )


def times_operator(rows, operator):
    half = rows.shape[1] // 4
    upper = jnp.concatenate([rows[:, half : 2 * half], rows[:, 3 * half :]], axis=1)
    lower = jnp.concatenate([rows[:, :half], rows[:, 2 * half : 3 * half]], axis=1)
    both = jnp.dot(
        jnp.concatenate([upper, lower], axis=0), operator, preferred_element_type=F32
    )
    scale = 1.0 / math.sqrt(2.0 * half)
    count = rows.shape[0]
    above = both[:count] * scale
    below = both[count:] * (-scale)
    return jnp.concatenate([above[:, :half], below[:, :half], above[:, half:], below[:, half:]], 1)


def times_rows(left, right):
    order = left.shape[1] // 2
    count = left.shape[0]
    both = jnp.dot(
        jnp.concatenate([left[:, :order], left[:, order:]], axis=0),
        right,
        preferred_element_type=F32,
    )
    real_part = both[:count, :order] - both[count:, order:]
    imag_part = both[:count, order:] + both[count:, :order]
    return real_part, imag_part


def diagonal_sum(part, first_row):
    row = lax.broadcasted_iota(jnp.int32, part.shape, 0) + first_row
    column = lax.broadcasted_iota(jnp.int32, part.shape, 1)
    kept = jnp.where(row == column, part, 0.0)
    return jnp.sum(jnp.sum(kept, axis=0, keepdims=True), axis=1, keepdims=True)


def at_lanes(shape, values):
    lane = lax.broadcasted_iota(jnp.int32, shape, 1)
    total = jnp.zeros(shape, F32)
    for at, value in values:
        total = total + jnp.where(lane == at, value, 0.0)
    return total


def own_block(spaces, spins, space_step, spin_step):
    place = lax.rem(lax.axis_index("space") + space_step, spaces)
    spin = lax.rem(lax.axis_index("spin") + spin_step, spins)
    return place * spins + spin


def first_kernel(spaces, spins, oper_ref, own_ref, *refs):
    block_refs, first_ref = refs[:-1], refs[-1]
    count = own_ref.shape[0]
    start = pl.multiple_of(own_block(spaces, spins, 0, 0) * count, count)
    first_ref[pl.ds(start, count), :] = own_ref[...]
    at = 1
    left = list(block_refs)
    while left:
        rows = left.pop(0)[...]
        while rows.shape[0] < count:
            rows = jnp.concatenate([rows, left.pop(0)[...]], axis=0)
        product = times_operator(rows, oper_ref[...])
        start = pl.multiple_of(own_block(spaces, spins, at // spins, at % spins) * count, count)
        first_ref[pl.ds(start, count), :] = product.astype(BF16)
        at += 1


def second_kernel(spaces, spins, next_ref, first_ref, early_ref, second_ref, trace_ref):
    count = next_ref.shape[0]
    order = next_ref.shape[1] // 2
    first_row = own_block(spaces, spins, 0, 0) * count
    real_part, imag_part = times_rows(next_ref[...], first_ref[...])
    second_ref[:, :order] = real_part.astype(BF16)
    second_ref[:, order:] = imag_part.astype(BF16)
    trace_ref[...] = early_ref[...] + at_lanes(
        trace_ref.shape,
        [(2, diagonal_sum(real_part, first_row)), (3, diagonal_sum(imag_part, first_row))],
    )


def third_kernel(spaces, spins, second_ref, first_ref, early_ref, chain_ref, trace_ref):
    count = second_ref.shape[0]
    order = second_ref.shape[1] // 2
    first_row = own_block(spaces, spins, 0, 0) * count
    real_part, imag_part = times_rows(second_ref[...], first_ref[...])
    scale = math.sqrt(order)
    chain_ref[:, :order] = (real_part * scale).astype(BF16)
    chain_ref[:, order:] = (imag_part * scale).astype(BF16)
    late = at_lanes(
        early_ref.shape,
        [(4, diagonal_sum(real_part, first_row)), (5, diagonal_sum(imag_part, first_row))],
    )
    row = lax.broadcasted_iota(jnp.int32, trace_ref.shape, 0)
    values = jnp.broadcast_to((early_ref[...] + late)[0:1], trace_ref.shape)
    trace_ref[...] = jnp.where(row == lax.axis_index("tm"), values, 0.0)


def correlator_kernel(offsets_ref, times_ref, *refs):
    part_refs, out_ref = refs[:-1], refs[-1]
    traces = part_refs[0][...]
    for part_ref in part_refs[1:]:
        traces = traces + part_ref[...]
    lane = lax.broadcasted_iota(jnp.int32, (1, traces.shape[1]), 1)
    counts = jnp.zeros((1, traces.shape[1]), F32)
    for j in range(offsets_ref.shape[0]):
        counts = counts + jnp.where(lane // 2 == offsets_ref[j], 1.0, 0.0)
    weighted = traces * counts
    row = lax.broadcasted_iota(jnp.int32, (traces.shape[0], times_ref.shape[1]), 0)
    chosen = row == times_ref[...]
    for part in range(2):
        keep = (lane % 2 == part) & (lane < 6)
        column = jnp.sum(jnp.where(keep, weighted, 0.0), axis=1, keepdims=True)
        out_ref[part : part + 1, :] = jnp.sum(
            jnp.where(chosen, column, 0.0), axis=0, keepdims=True
        )


def on_device(
    eigenvectors, gauge_links, perambulators, source_times, insert_offsets, derivative_dirs
):
    spaces, spins, slots = lax.axis_size("space"), lax.axis_size("spin"), lax.axis_size("tm")
    planes, side, modes = eigenvectors.shape[3], eigenvectors.shape[4], eigenvectors.shape[6]
    cells = planes * side * side
    own_rows = perambulators[0]
    count, width = own_rows.shape
    order = width // 2

    vectors = eigenvectors.reshape((6 * cells, modes))
    links = gauge_links.reshape((54, cells)).T
    links = jnp.pad(links, ((0, 0), (0, modes - 54)))
    pack = jnp.concatenate([vectors, links], axis=0)
    slabs = [pack] + [from_offset(pack, "space", step) for step in range(1, spaces)]
    far_rows = [from_offset(own_rows, "space", step) for step in range(1, spaces)]

    norm_scale = 1.0 / math.sqrt(6.0 * 4.0 * planes * spaces * side * side)
    rows_shape = jax.ShapeDtypeStruct((count, width), BF16)
    trace_shape = jax.ShapeDtypeStruct((8, 128), F32)
    elements, operator, own_first, early = vmem_call(
        functools.partial(elementals_kernel, cells, side, norm_scale, spaces, spins),
        (
            jax.ShapeDtypeStruct((3, 2, modes, modes), F32),
            jax.ShapeDtypeStruct((4 * modes, 4 * modes), BF16),
            rows_shape,
            trace_shape,
        ),
        [
            pltpu.VMEM((6 * cells * spaces, 6 * modes), BF16),
            pltpu.VMEM((3, 2, modes, modes), F32),
        ],
        10**10,
        smem=(0,),
    )(derivative_dirs, own_rows, *slabs)

    next_first = from_offset(own_first, "tm", 1)

    far_rows, held_first = lax.optimization_barrier((far_rows, own_first))
    blocks = []
    for at, block in enumerate([own_rows] + far_rows):
        blocks += [block]
        pieces = PIECES if at else 1
        for step in range(1, spins):
            for piece in range(pieces):
                low, high = piece * count // pieces, (piece + 1) * count // pieces
                blocks += [from_offset(block[low:high], "spin", step)]
    blocks = blocks[1:]
    first = vmem_call(
        functools.partial(first_kernel, spaces, spins),
        jax.ShapeDtypeStruct((order, width), BF16),
        [],
        10**6,
    )(operator, held_first, *blocks)

    second, early = vmem_call(
        functools.partial(second_kernel, spaces, spins),
        (rows_shape, trace_shape),
        [],
        3 * 10**8,
    )(next_first, first, early)

    next_second = from_offset(second, "tm", 1)

    rows, columns = modes // spaces, modes // spins
    share = lax.dynamic_slice(
        elements,
        (0, 0, lax.axis_index("space") * rows, lax.axis_index("spin") * columns),
        (3, 2, rows, columns),
    )
    elementals = jnp.transpose(share, (2, 0, 1, 3))

    chain, traces = vmem_call(
        functools.partial(third_kernel, spaces, spins),
        (
            jax.ShapeDtypeStruct((count, width), BF16),
            jax.ShapeDtypeStruct((-(-slots // 8) * 8, 128), F32),
        ),
        [],
        3 * 10**8,
    )(next_second, first, early)

    group = spaces * spins
    parts = [traces] + [from_offset(traces, ("space", "spin"), step) for step in range(1, group)]
    traces = functools.reduce(lambda a, b: a + b, parts)
    if slots & (slots - 1):
        parts = [lax.psum(traces, "tm")]
    else:
        step = 1
        while step < slots:
            other = lax.ppermute(traces, "tm", [(i ^ step, i) for i in range(slots)])
            parts = [traces, other]
            traces = traces + other
            step *= 2
    correlator = vmem_call(
        correlator_kernel,
        jax.ShapeDtypeStruct((2, source_times.shape[0]), F32),
        [],
        10**5,
        smem=(0,),
    )(insert_offsets, source_times[None, :], *parts)
    return (elementals[None], chain[None], correlator.T)


def solution(mesh):
    in_specs = (
        P(("cfg", "tm"), None, None, "space", None, None, None),
        P(("cfg", "tm"), None, None, None, None, "space", None),
        P(("cfg", "tm"), ("space", "spin"), None),
        P(),
        P(),
        P(),
    )
    out_specs = (
        P(("cfg", "tm"), "space", None, None, "spin"),
        P(("cfg", "tm"), ("space", "spin"), None),
        P("cfg", None),
    )
    return jax.shard_map(
        on_device, mesh=mesh, in_specs=in_specs, out_specs=out_specs, check_vma=False
    )
```

```python
import functools
import math

import jax
import jax.numpy as jnp
from jax import lax
from jax.experimental import pallas as pl
from jax.experimental.pallas import tpu as pltpu

from jax.sharding import PartitionSpec as P

F32 = jnp.float32
BF16 = jnp.bfloat16
PIECES = 2


def from_offset(block, axis, distance):
    count = lax.axis_size(axis)
    return lax.ppermute(block, axis, [((i + distance) % count, i) for i in range(count)])


def vmem_call(kernel, out_shape, scratch, flops, smem=()):
    def call(*operands):
        specs = [
            pl.BlockSpec(memory_space=pltpu.SMEM if i in smem else pltpu.VMEM)
            for i in range(len(operands))
        ]
        outs = jax.tree.map(lambda _: pl.BlockSpec(memory_space=pltpu.VMEM), out_shape)
        return pl.pallas_call(
            kernel,
            out_shape=out_shape,
            in_specs=specs,
            out_specs=outs,
            scratch_shapes=scratch,
            compiler_params=pltpu.CompilerParams(vmem_limit_bytes=16 * 1024 * 1024),
            cost_estimate=pl.CostEstimate(
                flops=flops, bytes_accessed=1 << 20, transcendentals=0
            ),
        )(*operands)

    return call


def moved(field, distance):
    rows = field.shape[0]
    return pltpu.roll(field, distance % rows, 0) if distance % rows else field


def ahead_of(field, stride, side):
    row = lax.broadcasted_iota(jnp.int32, field.shape, 0)
    last = (row // stride) % side == side - 1
    return jnp.where(last, moved(field, (side - 1) * stride), moved(field, -stride))


def behind_of(field, stride, side):
    row = lax.broadcasted_iota(jnp.int32, field.shape, 0)
    start = (row // stride) % side == 0
    return jnp.where(start, moved(field, (1 - side) * stride), moved(field, stride))


def site_links(links_ref, wide_ref, turned_ref):
    coefficients, cross, planes = links_ref.shape
    wide_ref[...] = links_ref[...].astype(F32)
    for at in range(cross):
        rows = pl.ds(at, planes, stride=cross)
        turned_ref[rows, :coefficients] = wide_ref[:, at, :].T
    return turned_ref[...]


def link_at(links, direction, colour, other):
    at = direction * 18 + colour * 3 + other
    return links[:, at : at + 1], links[:, at + 9 : at + 10]


def added(total, term):
    return term if total is None else total + term


def times_links(links, direction, vectors):
    parts = [None] * 6
    for colour in range(3):
        for other in range(3):
            real, imag = link_at(links, direction, colour, other)
            real_part, imag_part = vectors[other], vectors[3 + other]
            parts[colour] = added(parts[colour], real * real_part - imag * imag_part)
            parts[3 + colour] = added(parts[3 + colour], real * imag_part + imag * real_part)
    return parts


def times_adjoint(links, direction, vectors):
    parts = [None] * 6
    for colour in range(3):
        for other in range(3):
            real, imag = link_at(links, direction, colour, other)
            real_part, imag_part = vectors[colour], vectors[3 + colour]
            parts[other] = added(parts[other], real * real_part + imag * imag_part)
            parts[3 + other] = added(parts[3 + other], real * imag_part - imag * real_part)
    return [part.astype(BF16) for part in parts]


def across_slab(links, direction, vectors, side):
    stride = side**direction
    forward = times_links(links, direction, [ahead_of(v, stride, side) for v in vectors])
    adjoint = times_adjoint(links, direction, vectors)
    return [
        (part - behind_of(back.astype(F32), stride, side)).astype(BF16)
        for part, back in zip(forward, adjoint)
    ]


def slab_fields(ref):
    cells = ref.shape[0] // 6
    return [ref[k * cells : (k + 1) * cells, :].astype(F32) for k in range(6)]


def slab_kernel(side, vectors_ref, links_ref, copy_ref, turned_ref, out_ref, wide_ref):
    vectors = slab_fields(vectors_ref)
    links = site_links(links_ref, wide_ref, turned_ref)
    cells = links.shape[0]
    copy_ref[...] = vectors_ref[...]
    parts = across_slab(links, 0, vectors, side) + across_slab(links, 1, vectors, side)
    parts += times_adjoint(links, 2, vectors)
    for at, part in enumerate(parts):
        out_ref[at * cells : (at + 1) * cells, :] = part


def elementals_kernel(side, scale, slabs, early_ref, *refs):
    vector_refs, link_refs, out_refs = refs[:slabs], refs[slabs : 2 * slabs], refs[2 * slabs :]
    elem_ref, rhs_ref, wide_ref, turned_ref = out_refs
    modes = elem_ref.shape[-1]
    cells = link_refs[0].shape[0]
    sites = slabs * cells

    def put(slab, direction, parts):
        left, right = 2 * direction * modes, (2 * direction + 1) * modes
        for colour in range(3):
            low = colour * sites + slab * cells
            high = low + 3 * sites
            real_part, imag_part = parts[colour], parts[3 + colour]
            rhs_ref[low : low + cells, left : left + modes] = real_part
            rhs_ref[high : high + cells, left : left + modes] = imag_part
            rhs_ref[low : low + cells, right : right + modes] = imag_part
            rhs_ref[high : high + cells, right : right + modes] = -real_part

    early = [early_ref[at * cells : (at + 1) * cells, :] for at in range(18)]
    put(0, 0, early[:6])
    put(0, 1, early[6:12])
    vectors = [slab_fields(ref) for ref in vector_refs]
    links = [link_refs[0][...]]
    links += [
        site_links(ref, wide_ref.at[at], turned_ref.at[at])
        for at, ref in enumerate(link_refs[1:])
    ]
    adjoint = [early[12:]]
    for slab in range(1, slabs):
        put(slab, 0, across_slab(links[slab], 0, vectors[slab], side))
        put(slab, 1, across_slab(links[slab], 1, vectors[slab], side))
        adjoint.append(times_adjoint(links[slab], 2, vectors[slab]))
    plane = side * side
    for slab in range(slabs):
        after, before = (slab + 1) % slabs, (slab - 1) % slabs
        ahead = [
            jnp.concatenate([here[plane:], there[:plane]], axis=0)
            for here, there in zip(vectors[slab], vectors[after])
        ]
        forward = times_links(links[slab], 2, ahead)
        parts = []
        for k in range(6):
            here, there = adjoint[slab][k].astype(F32), adjoint[before][k].astype(F32)
            behind = jnp.concatenate([there[cells - plane :], here[: cells - plane]], axis=0)
            parts.append((forward[k] - behind).astype(BF16))
        put(slab, 2, parts)

    fields = [ref[k * cells : (k + 1) * cells, :] for k in range(6) for ref in vector_refs]
    vectors = jnp.concatenate(fields, axis=0)
    product = lax.dot_general(
        vectors, rhs_ref[...], (((0,), (0,)), ((), ())), preferred_element_type=F32
    )
    for direction in range(3):
        left = 2 * direction * modes
        real_part = product[:, left : left + modes] * scale
        imag_part = product[:, left + modes : left + 2 * modes] * scale
        elem_ref[direction, 0] = real_part
        elem_ref[direction, 1] = imag_part


def operator_kernel(
    spaces, spins, dirs_ref, elem_ref, rows_ref, oper_ref, first_ref, trace_ref, copy_ref
):
    modes = elem_ref.shape[-1]
    copy_ref[...] = rows_ref[...]
    picked = []
    for k in range(3):
        for part in range(2):
            picked.append(elem_ref[dirs_ref[k], part].astype(BF16).astype(F32))
    zero_real, zero_imag, one_real, one_imag, two_real, two_imag = picked
    sum_real = [[two_real, zero_real + one_imag], [zero_real - one_imag, -two_real]]
    sum_imag = [[two_imag, zero_imag - one_real], [zero_imag + one_real, -two_imag]]
    for p in range(2):
        for q in range(2):
            top, bottom = p * modes, (2 + p) * modes
            left, right = q * modes, (2 + q) * modes
            real_part = sum_real[p][q].astype(BF16)
            imag_part = sum_imag[p][q].astype(BF16)
            oper_ref[top : top + modes, left : left + modes] = -imag_part
            oper_ref[top : top + modes, right : right + modes] = real_part
            oper_ref[bottom : bottom + modes, left : left + modes] = -real_part
            oper_ref[bottom : bottom + modes, right : right + modes] = -imag_part
    count, width = rows_ref.shape
    first_row = own_block(spaces, spins, 0, 0) * count
    product = times_operator(rows_ref[...], oper_ref[...])
    first_ref[...] = product.astype(BF16)
    trace_ref[...] = at_lanes(
        trace_ref.shape,
        [
            (0, diagonal_sum(product[:, : width // 2], first_row)),
            (1, diagonal_sum(product[:, width // 2 :], first_row)),
        ],
    )


def times_operator(rows, operator):
    half = rows.shape[1] // 4
    upper = jnp.concatenate([rows[:, half : 2 * half], rows[:, 3 * half :]], axis=1)
    lower = jnp.concatenate([rows[:, :half], rows[:, 2 * half : 3 * half]], axis=1)
    both = jnp.dot(
        jnp.concatenate([upper, lower], axis=0), operator, preferred_element_type=F32
    )
    scale = 1.0 / math.sqrt(2.0 * half)
    count = rows.shape[0]
    above = both[:count] * scale
    below = both[count:] * (-scale)
    return jnp.concatenate([above[:, :half], below[:, :half], above[:, half:], below[:, half:]], 1)


def times_rows(left, right):
    order = left.shape[1] // 2
    count = left.shape[0]
    both = jnp.dot(
        jnp.concatenate([left[:, :order], left[:, order:]], axis=0),
        right,
        preferred_element_type=F32,
    )
    real_part = both[:count, :order] - both[count:, order:]
    imag_part = both[:count, order:] + both[count:, :order]
    return real_part, imag_part


def diagonal_sum(part, first_row):
    row = lax.broadcasted_iota(jnp.int32, part.shape, 0) + first_row
    column = lax.broadcasted_iota(jnp.int32, part.shape, 1)
    kept = jnp.where(row == column, part, 0.0)
    return jnp.sum(jnp.sum(kept, axis=0, keepdims=True), axis=1, keepdims=True)


def at_lanes(shape, values):
    lane = lax.broadcasted_iota(jnp.int32, shape, 1)
    total = jnp.zeros(shape, F32)
    for at, value in values:
        total = total + jnp.where(lane == at, value, 0.0)
    return total


def own_block(spaces, spins, space_step, spin_step):
    place = lax.rem(lax.axis_index("space") + space_step, spaces)
    spin = lax.rem(lax.axis_index("spin") + spin_step, spins)
    return place * spins + spin


def first_kernel(spaces, spins, oper_ref, own_ref, *refs):
    block_refs, first_ref = refs[:-1], refs[-1]
    count = own_ref.shape[0]
    start = pl.multiple_of(own_block(spaces, spins, 0, 0) * count, count)
    first_ref[pl.ds(start, count), :] = own_ref[...]
    at = 1
    left = list(block_refs)
    while left:
        rows = left.pop(0)[...]
        while rows.shape[0] < count:
            rows = jnp.concatenate([rows, left.pop(0)[...]], axis=0)
        product = times_operator(rows, oper_ref[...])
        start = pl.multiple_of(own_block(spaces, spins, at // spins, at % spins) * count, count)
        first_ref[pl.ds(start, count), :] = product.astype(BF16)
        at += 1


def second_kernel(spaces, spins, next_ref, first_ref, early_ref, second_ref, trace_ref):
    count = next_ref.shape[0]
    order = next_ref.shape[1] // 2
    first_row = own_block(spaces, spins, 0, 0) * count
    real_part, imag_part = times_rows(next_ref[...], first_ref[...])
    second_ref[:, :order] = real_part.astype(BF16)
    second_ref[:, order:] = imag_part.astype(BF16)
    trace_ref[...] = early_ref[...] + at_lanes(
        trace_ref.shape,
        [(2, diagonal_sum(real_part, first_row)), (3, diagonal_sum(imag_part, first_row))],
    )


def turn_kernel(spaces, spins, offsets_ref, times_ref, first_ref, elem_ref, *refs):
    out_ref, weights_ref, share_ref, wide_ref = refs
    count, width = out_ref.shape
    order, lanes = width // 2, wide_ref.shape[0]
    first_row = own_block(spaces, spins, 0, 0) * count
    start = pl.multiple_of(first_row // lanes * lanes, lanes)
    for part in range(2):
        block = first_ref[:, pl.ds(pl.multiple_of(start + part * order, lanes), lanes)]
        wide_ref[:, part * order : (part + 1) * order] = block.astype(F32).T
    rows = pl.ds(pl.multiple_of(first_row - start, count), count)
    out_ref[...] = wide_ref[rows, :].astype(BF16)
    lane = lax.broadcasted_iota(jnp.int32, weights_ref.shape, 1)
    row = lax.broadcasted_iota(jnp.int32, weights_ref.shape, 0)
    counts = jnp.zeros(weights_ref.shape, F32)
    for j in range(offsets_ref.shape[0]):
        counts = counts + jnp.where(lane // 2 == offsets_ref[j], 1.0, 0.0)
    counts = jnp.where((lane < 6) & (lane % 2 == row), counts, 0.0)
    weights_ref[...] = counts
    here = jnp.where(times_ref[...] == lax.axis_index("tm"), 1.0, 0.0)
    weights_ref[2:3, : here.shape[1]] = here
    rows, columns = share_ref.shape[0], share_ref.shape[3]
    modes = elem_ref.shape[3]
    top = pl.multiple_of(lax.axis_index("space") * rows, rows)
    turn = lax.rem(modes - lax.axis_index("spin") * columns, modes)
    for direction in range(3):
        for part in range(2):
            block = elem_ref[direction, part, pl.ds(top, rows), :]
            share_ref[:, direction, part, :] = pltpu.roll(block, turn, 1)[:, :columns]


def whole_sum(values):
    return jnp.sum(jnp.sum(values, axis=0, keepdims=True), axis=1, keepdims=True)


def share_kernel(weights_ref, second_ref, turned_ref, early_ref, out_ref):
    order = second_ref.shape[1] // 2
    left_real, left_imag = second_ref[:, :order].astype(F32), second_ref[:, order:].astype(F32)
    right_real, right_imag = turned_ref[:, :order].astype(F32), turned_ref[:, order:].astype(F32)
    real_part = whole_sum(left_real * right_real - left_imag * right_imag)
    imag_part = whole_sum(left_real * right_imag + left_imag * right_real)
    traces = early_ref[0:1, :] + at_lanes((1, 128), [(4, real_part), (5, imag_part)])
    values = jnp.sum(traces * weights_ref[0:2, :], axis=1, keepdims=True)
    out_ref[...] = values * weights_ref[2:3, : out_ref.shape[1]]


def third_kernel(second_ref, first_ref, chain_ref):
    order = second_ref.shape[1] // 2
    real_part, imag_part = times_rows(second_ref[...], first_ref[...])
    scale = math.sqrt(order)
    chain_ref[:, :order] = (real_part * scale).astype(BF16)
    chain_ref[:, order:] = (imag_part * scale).astype(BF16)


def on_device(
    eigenvectors, gauge_links, perambulators, source_times, insert_offsets, derivative_dirs
):
    spaces, spins, slots = lax.axis_size("space"), lax.axis_size("spin"), lax.axis_size("tm")
    planes, side, modes = eigenvectors.shape[3], eigenvectors.shape[4], eigenvectors.shape[6]
    cells = planes * side * side
    own_rows = perambulators[0]
    count, width = own_rows.shape
    order = width // 2

    field = eigenvectors.reshape((6 * cells, modes))
    fields = [field] + [from_offset(field, "space", step) for step in range(1, spaces)]
    link = jnp.swapaxes(gauge_links.reshape((54, planes, side * side)), 1, 2)
    links = [link] + [from_offset(link, "space", step) for step in range(1, spaces)]
    far_rows = [from_offset(own_rows, "space", step) for step in range(1, spaces)]
    fields[0], links[0], own_slab = vmem_call(
        functools.partial(slab_kernel, side),
        (
            jax.ShapeDtypeStruct(field.shape, BF16),
            jax.ShapeDtypeStruct((cells, modes), F32),
            jax.ShapeDtypeStruct((18 * cells, modes), BF16),
        ),
        [pltpu.VMEM(link.shape, F32)],
        10**6,
    )(field, link)

    norm_scale = 1.0 / math.sqrt(6.0 * 4.0 * planes * spaces * side * side)
    rows_shape = jax.ShapeDtypeStruct((count, width), BF16)
    trace_shape = jax.ShapeDtypeStruct((8, 128), F32)
    elements = vmem_call(
        functools.partial(elementals_kernel, side, norm_scale, spaces),
        jax.ShapeDtypeStruct((3, 2, modes, modes), F32),
        [
            pltpu.VMEM((6 * cells * spaces, 6 * modes), BF16),
            pltpu.VMEM((spaces - 1,) + link.shape, F32),
            pltpu.VMEM((spaces - 1, cells, modes), F32),
        ],
        10**10,
    )(own_slab, *fields, *links)
    operator, own_first, early, rows_copy = vmem_call(
        functools.partial(operator_kernel, spaces, spins),
        (
            jax.ShapeDtypeStruct((4 * modes, 4 * modes), BF16),
            rows_shape,
            trace_shape,
            rows_shape,
        ),
        [],
        10**8,
        smem=(0,),
    )(derivative_dirs, elements, own_rows)

    next_first = from_offset(own_first, "tm", 1)

    far_rows, held_rows, held_first = lax.optimization_barrier((far_rows, rows_copy, own_first))
    blocks = []
    for at, block in enumerate([held_rows] + far_rows):
        blocks += [block]
        pieces = PIECES if at else 1
        for step in range(1, spins):
            for piece in range(pieces):
                low, high = piece * count // pieces, (piece + 1) * count // pieces
                blocks += [from_offset(block[low:high], "spin", step)]
    blocks = blocks[1:]
    first = vmem_call(
        functools.partial(first_kernel, spaces, spins),
        jax.ShapeDtypeStruct((order, width), BF16),
        [],
        10**6,
    )(operator, held_first, *blocks)

    second, early = vmem_call(
        functools.partial(second_kernel, spaces, spins),
        (rows_shape, trace_shape),
        [],
        3 * 10**8,
    )(next_first, first, early)

    next_second = from_offset(second, "tm", 1)

    turned, weights, elementals = vmem_call(
        functools.partial(turn_kernel, spaces, spins),
        (
            rows_shape,
            trace_shape,
            jax.ShapeDtypeStruct((modes // spaces, 3, 2, modes // spins), F32),
        ),
        [pltpu.VMEM((max(count, 128), width), F32)],
        10**6,
        smem=(0,),
    )(insert_offsets, source_times[None, :], first, elements)
    shares = vmem_call(
        share_kernel,
        jax.ShapeDtypeStruct((2, source_times.shape[0]), F32),
        [],
        10**6,
    )(weights, next_second, turned, early)
    chain = vmem_call(third_kernel, rows_shape, [], 10**8)(next_second, first)

    group = spaces * spins
    parts = [shares] + [from_offset(shares, ("space", "spin"), step) for step in range(1, group)]
    shares = functools.reduce(lambda a, b: a + b, parts)
    shares, chain = lax.optimization_barrier((shares, chain))
    if slots & (slots - 1):
        shares = lax.psum(shares, "tm")
    else:
        step = 1
        while step < slots:
            shares = shares + lax.ppermute(shares, "tm", [(i ^ step, i) for i in range(slots)])
            step *= 2
    return (elementals[None], chain[None], shares.T)


def solution(mesh):
    in_specs = (
        P(("cfg", "tm"), None, None, "space", None, None, None),
        P(("cfg", "tm"), None, None, None, None, "space", None),
        P(("cfg", "tm"), ("space", "spin"), None),
        P(),
        P(),
        P(),
    )
    out_specs = (
        P(("cfg", "tm"), "space", None, None, "spin"),
        P(("cfg", "tm"), ("space", "spin"), None),
        P("cfg", None),
    )
    return jax.shard_map(
        on_device, mesh=mesh, in_specs=in_specs, out_specs=out_specs, check_vma=False
    )
```

```python
import functools
import math

import jax
import jax.numpy as jnp
from jax import lax
from jax.experimental import pallas as pl
from jax.experimental.pallas import tpu as pltpu

from jax.sharding import PartitionSpec as P

F32 = jnp.float32
BF16 = jnp.bfloat16
PIECES = 2


def from_offset(block, axis, distance):
    count = lax.axis_size(axis)
    return lax.ppermute(block, axis, [((i + distance) % count, i) for i in range(count)])


def vmem_call(kernel, out_shape, scratch, flops, smem=()):
    def call(*operands):
        specs = [
            pl.BlockSpec(memory_space=pltpu.SMEM if i in smem else pltpu.VMEM)
            for i in range(len(operands))
        ]
        outs = jax.tree.map(lambda _: pl.BlockSpec(memory_space=pltpu.VMEM), out_shape)
        return pl.pallas_call(
            kernel,
            out_shape=out_shape,
            in_specs=specs,
            out_specs=outs,
            scratch_shapes=scratch,
            compiler_params=pltpu.CompilerParams(vmem_limit_bytes=16 * 1024 * 1024),
            cost_estimate=pl.CostEstimate(
                flops=flops, bytes_accessed=1 << 20, transcendentals=0
            ),
        )(*operands)

    return call


def moved(field, distance):
    rows = field.shape[0]
    return pltpu.roll(field, distance % rows, 0) if distance % rows else field


def ahead_of(field, stride, side):
    row = lax.broadcasted_iota(jnp.int32, field.shape, 0)
    last = (row // stride) % side == side - 1
    return jnp.where(last, moved(field, (side - 1) * stride), moved(field, -stride))


def behind_of(field, stride, side):
    row = lax.broadcasted_iota(jnp.int32, field.shape, 0)
    start = (row // stride) % side == 0
    return jnp.where(start, moved(field, (1 - side) * stride), moved(field, stride))


def links_kernel(links_ref, out_ref, wide_ref, turned_ref):
    coefficients, cross, planes = links_ref.shape
    wide_ref[...] = links_ref[...].astype(F32)
    for at in range(cross):
        rows = pl.ds(at, planes, stride=cross)
        turned_ref[rows, :coefficients] = wide_ref[:, at, :].T
    out_ref[...] = turned_ref[...].astype(BF16)


def link_at(links, direction, colour, other):
    at = direction * 18 + colour * 3 + other
    return links[:, at : at + 1], links[:, at + 9 : at + 10]


def added(total, term):
    return term if total is None else total + term


def times_links(links, direction, vectors):
    parts = [None] * 6
    for colour in range(3):
        for other in range(3):
            real, imag = link_at(links, direction, colour, other)
            real_part, imag_part = vectors[other], vectors[3 + other]
            parts[colour] = added(parts[colour], real * real_part - imag * imag_part)
            parts[3 + colour] = added(parts[3 + colour], real * imag_part + imag * real_part)
    return parts


def times_adjoint(links, direction, vectors):
    parts = [None] * 6
    for colour in range(3):
        for other in range(3):
            real, imag = link_at(links, direction, colour, other)
            real_part, imag_part = vectors[colour], vectors[3 + colour]
            parts[other] = added(parts[other], real * real_part + imag * imag_part)
            parts[3 + other] = added(parts[3 + other], real * imag_part - imag * real_part)
    return [part.astype(BF16) for part in parts]


def across_slab(links, direction, vectors, side):
    stride = side**direction
    forward = times_links(links, direction, [ahead_of(v, stride, side) for v in vectors])
    adjoint = times_adjoint(links, direction, vectors)
    return [
        (part - behind_of(back.astype(F32), stride, side)).astype(BF16)
        for part, back in zip(forward, adjoint)
    ]


def slab_fields(ref):
    cells = ref.shape[0] // 6
    return [ref[k * cells : (k + 1) * cells, :].astype(F32) for k in range(6)]


def slab_kernel(side, vectors_ref, links_ref, copy_ref, out_ref):
    vectors = slab_fields(vectors_ref)
    links = links_ref[...].astype(F32)
    cells = links.shape[0]
    copy_ref[...] = vectors_ref[...]
    parts = across_slab(links, 0, vectors, side) + across_slab(links, 1, vectors, side)
    parts += times_adjoint(links, 2, vectors)
    for at, part in enumerate(parts):
        out_ref[at * cells : (at + 1) * cells, :] = part


def elementals_kernel(side, scale, slabs, early_ref, *refs):
    vector_refs, link_refs, out_refs = refs[:slabs], refs[slabs : 2 * slabs], refs[2 * slabs :]
    elem_ref, rhs_ref = out_refs
    modes = elem_ref.shape[-1]
    cells = link_refs[0].shape[0]
    sites = slabs * cells

    def put(slab, direction, parts):
        left, right = 2 * direction * modes, (2 * direction + 1) * modes
        for colour in range(3):
            low = colour * sites + slab * cells
            high = low + 3 * sites
            real_part, imag_part = parts[colour], parts[3 + colour]
            rhs_ref[low : low + cells, left : left + modes] = real_part
            rhs_ref[high : high + cells, left : left + modes] = imag_part
            rhs_ref[low : low + cells, right : right + modes] = imag_part
            rhs_ref[high : high + cells, right : right + modes] = -real_part

    early = [early_ref[at * cells : (at + 1) * cells, :] for at in range(18)]
    put(0, 0, early[:6])
    put(0, 1, early[6:12])
    vectors = [slab_fields(ref) for ref in vector_refs]
    links = [ref[...].astype(F32) for ref in link_refs]
    adjoint = [early[12:]]
    for slab in range(1, slabs):
        put(slab, 0, across_slab(links[slab], 0, vectors[slab], side))
        put(slab, 1, across_slab(links[slab], 1, vectors[slab], side))
        adjoint.append(times_adjoint(links[slab], 2, vectors[slab]))
    plane = side * side
    for slab in range(slabs):
        after, before = (slab + 1) % slabs, (slab - 1) % slabs
        ahead = [
            jnp.concatenate([here[plane:], there[:plane]], axis=0)
            for here, there in zip(vectors[slab], vectors[after])
        ]
        forward = times_links(links[slab], 2, ahead)
        parts = []
        for k in range(6):
            here, there = adjoint[slab][k].astype(F32), adjoint[before][k].astype(F32)
            behind = jnp.concatenate([there[cells - plane :], here[: cells - plane]], axis=0)
            parts.append((forward[k] - behind).astype(BF16))
        put(slab, 2, parts)

    fields = [ref[k * cells : (k + 1) * cells, :] for k in range(6) for ref in vector_refs]
    vectors = jnp.concatenate(fields, axis=0)
    product = lax.dot_general(
        vectors, rhs_ref[...], (((0,), (0,)), ((), ())), preferred_element_type=F32
    )
    for direction in range(3):
        left = 2 * direction * modes
        real_part = product[:, left : left + modes] * scale
        imag_part = product[:, left + modes : left + 2 * modes] * scale
        elem_ref[direction, 0] = real_part
        elem_ref[direction, 1] = imag_part


def operator_kernel(
    dirs_ref, elem_ref, rows_ref, oper_ref, first_ref, wide_ref, copy_ref
):
    modes = elem_ref.shape[-1]
    copy_ref[...] = rows_ref[...]
    picked = []
    for k in range(3):
        for part in range(2):
            picked.append(elem_ref[dirs_ref[k], part].astype(BF16).astype(F32))
    zero_real, zero_imag, one_real, one_imag, two_real, two_imag = picked
    sum_real = [[two_real, zero_real + one_imag], [zero_real - one_imag, -two_real]]
    sum_imag = [[two_imag, zero_imag - one_real], [zero_imag + one_real, -two_imag]]
    for p in range(2):
        for q in range(2):
            top, bottom = p * modes, (2 + p) * modes
            left, right = q * modes, (2 + q) * modes
            real_part = sum_real[p][q].astype(BF16)
            imag_part = sum_imag[p][q].astype(BF16)
            oper_ref[top : top + modes, left : left + modes] = -imag_part
            oper_ref[top : top + modes, right : right + modes] = real_part
            oper_ref[bottom : bottom + modes, left : left + modes] = -real_part
            oper_ref[bottom : bottom + modes, right : right + modes] = -imag_part
    product = times_operator(rows_ref[...], oper_ref[...])
    first_ref[...] = product.astype(BF16)
    wide_ref[...] = product


def times_operator(rows, operator):
    half = rows.shape[1] // 4
    upper = jnp.concatenate([rows[:, half : 2 * half], rows[:, 3 * half :]], axis=1)
    lower = jnp.concatenate([rows[:, :half], rows[:, 2 * half : 3 * half]], axis=1)
    both = jnp.dot(
        jnp.concatenate([upper, lower], axis=0), operator, preferred_element_type=F32
    )
    scale = 1.0 / math.sqrt(2.0 * half)
    count = rows.shape[0]
    above = both[:count] * scale
    below = both[count:] * (-scale)
    return jnp.concatenate([above[:, :half], below[:, :half], above[:, half:], below[:, half:]], 1)


def times_rows(left, right):
    order = left.shape[1] // 2
    count = left.shape[0]
    both = jnp.dot(
        jnp.concatenate([left[:, :order], left[:, order:]], axis=0),
        right,
        preferred_element_type=F32,
    )
    real_part = both[:count, :order] - both[count:, order:]
    imag_part = both[:count, order:] + both[count:, :order]
    return real_part, imag_part


def diagonal_sum(part, first_row):
    row = lax.broadcasted_iota(jnp.int32, part.shape, 0) + first_row
    column = lax.broadcasted_iota(jnp.int32, part.shape, 1)
    kept = jnp.where(row == column, part, 0.0)
    return jnp.sum(jnp.sum(kept, axis=0, keepdims=True), axis=1, keepdims=True)


def at_lanes(shape, values):
    lane = lax.broadcasted_iota(jnp.int32, shape, 1)
    total = jnp.zeros(shape, F32)
    for at, value in values:
        total = total + jnp.where(lane == at, value, 0.0)
    return total


def own_block(spaces, spins, space_step, spin_step):
    place = lax.rem(lax.axis_index("space") + space_step, spaces)
    spin = lax.rem(lax.axis_index("spin") + spin_step, spins)
    return place * spins + spin


def first_kernel(spaces, spins, oper_ref, own_ref, *refs):
    block_refs, first_ref = refs[:-1], refs[-1]
    count = own_ref.shape[0]
    start = pl.multiple_of(own_block(spaces, spins, 0, 0) * count, count)
    first_ref[pl.ds(start, count), :] = own_ref[...]
    at = 1
    left = list(block_refs)
    while left:
        rows = left.pop(0)[...]
        while rows.shape[0] < count:
            rows = jnp.concatenate([rows, left.pop(0)[...]], axis=0)
        product = times_operator(rows, oper_ref[...])
        start = pl.multiple_of(own_block(spaces, spins, at // spins, at % spins) * count, count)
        first_ref[pl.ds(start, count), :] = product.astype(BF16)
        at += 1


def second_kernel(next_ref, first_ref, second_ref, wide_ref):
    order = next_ref.shape[1] // 2
    real_part, imag_part = times_rows(next_ref[...], first_ref[...])
    second_ref[:, :order] = real_part.astype(BF16)
    second_ref[:, order:] = imag_part.astype(BF16)
    wide_ref[:, :order] = real_part
    wide_ref[:, order:] = imag_part


def turn_kernel(spaces, spins, offsets_ref, times_ref, first_ref, elem_ref, *refs):
    one_ref, two_ref, out_ref, weights_ref, share_ref, trace_ref, wide_ref = refs
    count, width = out_ref.shape
    order, lanes = width // 2, wide_ref.shape[0]
    first_row = own_block(spaces, spins, 0, 0) * count
    start = pl.multiple_of(first_row // lanes * lanes, lanes)
    for part in range(2):
        block = first_ref[:, pl.ds(pl.multiple_of(start + part * order, lanes), lanes)]
        wide_ref[:, part * order : (part + 1) * order] = block.astype(F32).T
    rows = pl.ds(pl.multiple_of(first_row - start, count), count)
    out_ref[...] = wide_ref[rows, :].astype(BF16)
    values = []
    for at, part_ref in enumerate((one_ref, two_ref)):
        values.append((2 * at, diagonal_sum(part_ref[:, :order], first_row)))
        values.append((2 * at + 1, diagonal_sum(part_ref[:, order:], first_row)))
    trace_ref[...] = at_lanes(trace_ref.shape, values)
    lane = lax.broadcasted_iota(jnp.int32, weights_ref.shape, 1)
    row = lax.broadcasted_iota(jnp.int32, weights_ref.shape, 0)
    counts = jnp.zeros(weights_ref.shape, F32)
    for j in range(offsets_ref.shape[0]):
        counts = counts + jnp.where(lane // 2 == offsets_ref[j], 1.0, 0.0)
    counts = jnp.where((lane < 6) & (lane % 2 == row), counts, 0.0)
    weights_ref[...] = counts
    here = jnp.where(times_ref[...] == lax.axis_index("tm"), 1.0, 0.0)
    weights_ref[2:3, : here.shape[1]] = here
    rows, columns = share_ref.shape[0], share_ref.shape[3]
    modes = elem_ref.shape[3]
    top = pl.multiple_of(lax.axis_index("space") * rows, rows)
    turn = lax.rem(modes - lax.axis_index("spin") * columns, modes)
    for direction in range(3):
        for part in range(2):
            block = elem_ref[direction, part, pl.ds(top, rows), :]
            share_ref[:, direction, part, :] = pltpu.roll(block, turn, 1)[:, :columns]


def whole_sum(values):
    return jnp.sum(jnp.sum(values, axis=0, keepdims=True), axis=1, keepdims=True)


def share_kernel(weights_ref, second_ref, turned_ref, early_ref, out_ref):
    order = second_ref.shape[1] // 2
    left_real, left_imag = second_ref[:, :order].astype(F32), second_ref[:, order:].astype(F32)
    right_real, right_imag = turned_ref[:, :order].astype(F32), turned_ref[:, order:].astype(F32)
    real_part = whole_sum(left_real * right_real - left_imag * right_imag)
    imag_part = whole_sum(left_real * right_imag + left_imag * right_real)
    traces = early_ref[0:1, :] + at_lanes((1, 128), [(4, real_part), (5, imag_part)])
    values = jnp.sum(traces * weights_ref[0:2, :], axis=1, keepdims=True)
    out_ref[...] = values * weights_ref[2:3, : out_ref.shape[1]]


def third_kernel(second_ref, first_ref, chain_ref):
    order = second_ref.shape[1] // 2
    real_part, imag_part = times_rows(second_ref[...], first_ref[...])
    scale = math.sqrt(order)
    chain_ref[:, :order] = (real_part * scale).astype(BF16)
    chain_ref[:, order:] = (imag_part * scale).astype(BF16)


def on_device(
    eigenvectors, gauge_links, perambulators, source_times, insert_offsets, derivative_dirs
):
    spaces, spins, slots = lax.axis_size("space"), lax.axis_size("spin"), lax.axis_size("tm")
    planes, side, modes = eigenvectors.shape[3], eigenvectors.shape[4], eigenvectors.shape[6]
    cells = planes * side * side
    own_rows = perambulators[0]
    count, width = own_rows.shape
    order = width // 2

    field = eigenvectors.reshape((6 * cells, modes))
    fields = [field] + [from_offset(field, "space", step) for step in range(1, spaces)]
    link = jnp.swapaxes(gauge_links.reshape((54, planes, side * side)), 1, 2)
    link = vmem_call(
        links_kernel,
        jax.ShapeDtypeStruct((cells, modes), BF16),
        [pltpu.VMEM(link.shape, F32), pltpu.VMEM((cells, modes), F32)],
        10**6,
    )(link)
    links = [link] + [from_offset(link, "space", step) for step in range(1, spaces)]
    fields[0], own_slab = vmem_call(
        functools.partial(slab_kernel, side),
        (
            jax.ShapeDtypeStruct(field.shape, BF16),
            jax.ShapeDtypeStruct((18 * cells, modes), BF16),
        ),
        [],
        10**6,
    )(field, link)

    held_rows, own_slab = lax.optimization_barrier((own_rows, own_slab))
    far_rows = [from_offset(held_rows, "space", step) for step in range(1, spaces)]

    norm_scale = 1.0 / math.sqrt(6.0 * 4.0 * planes * spaces * side * side)
    rows_shape = jax.ShapeDtypeStruct((count, width), BF16)
    trace_shape = jax.ShapeDtypeStruct((8, 128), F32)
    elements = vmem_call(
        functools.partial(elementals_kernel, side, norm_scale, spaces),
        jax.ShapeDtypeStruct((3, 2, modes, modes), F32),
        [pltpu.VMEM((6 * cells * spaces, 6 * modes), BF16)],
        10**10,
    )(own_slab, *fields, *links)
    wide_shape = jax.ShapeDtypeStruct((count, width), F32)
    operator, own_first, own_wide, rows_copy = vmem_call(
        operator_kernel,
        (jax.ShapeDtypeStruct((4 * modes, 4 * modes), BF16), rows_shape, wide_shape, rows_shape),
        [],
        10**8,
        smem=(0,),
    )(derivative_dirs, elements, own_rows)

    next_first = from_offset(own_first, "tm", 1)

    far_rows, held_rows, held_first = lax.optimization_barrier((far_rows, rows_copy, own_first))
    blocks = []
    for at, block in enumerate([held_rows] + far_rows):
        blocks += [block]
        pieces = PIECES if at else 1
        for step in range(1, spins):
            for piece in range(pieces):
                low, high = piece * count // pieces, (piece + 1) * count // pieces
                blocks += [from_offset(block[low:high], "spin", step)]
    blocks = blocks[1:]
    first = vmem_call(
        functools.partial(first_kernel, spaces, spins),
        jax.ShapeDtypeStruct((order, width), BF16),
        [],
        10**6,
    )(operator, held_first, *blocks)

    second, second_wide = vmem_call(
        second_kernel,
        (rows_shape, wide_shape),
        [],
        3 * 10**8,
    )(next_first, first)

    next_second = from_offset(second, "tm", 1)

    turned, weights, elementals, early = vmem_call(
        functools.partial(turn_kernel, spaces, spins),
        (
            rows_shape,
            trace_shape,
            jax.ShapeDtypeStruct((modes // spaces, 3, 2, modes // spins), F32),
            trace_shape,
        ),
        [pltpu.VMEM((max(count, 128), width), F32)],
        10**6,
        smem=(0,),
    )(insert_offsets, source_times[None, :], first, elements, own_wide, second_wide)
    shares = vmem_call(
        share_kernel,
        jax.ShapeDtypeStruct((2, source_times.shape[0]), F32),
        [],
        10**6,
    )(weights, next_second, turned, early)
    chain = vmem_call(third_kernel, rows_shape, [], 10**8)(next_second, first)

    group = spaces * spins
    parts = [shares] + [from_offset(shares, ("space", "spin"), step) for step in range(1, group)]
    shares = functools.reduce(lambda a, b: a + b, parts)
    shares, chain = lax.optimization_barrier((shares, chain))
    if slots & (slots - 1):
        shares = lax.psum(shares, "tm")
    else:
        step = 1
        while step < slots:
            shares = shares + lax.ppermute(shares, "tm", [(i ^ step, i) for i in range(slots)])
            step *= 2
    return (elementals[None], chain[None], shares.T)


def solution(mesh):
    in_specs = (
        P(("cfg", "tm"), None, None, "space", None, None, None),
        P(("cfg", "tm"), None, None, None, None, "space", None),
        P(("cfg", "tm"), ("space", "spin"), None),
        P(),
        P(),
        P(),
    )
    out_specs = (
        P(("cfg", "tm"), "space", None, None, "spin"),
        P(("cfg", "tm"), ("space", "spin"), None),
        P("cfg", None),
    )
    return jax.shard_map(
        on_device, mesh=mesh, in_specs=in_specs, out_specs=out_specs, check_vma=False
    )
```

```python
import functools
import math

import jax
import jax.numpy as jnp
from jax import lax
from jax.experimental import pallas as pl
from jax.experimental.pallas import tpu as pltpu

from jax.sharding import PartitionSpec as P

F32 = jnp.float32
BF16 = jnp.bfloat16
PIECES = 2


def from_offset(block, axis, distance):
    count = lax.axis_size(axis)
    return lax.ppermute(block, axis, [((i + distance) % count, i) for i in range(count)])


def swapped(block, devices, mask):
    return lax.ppermute(block, ("tm", "space", "spin"), [(i ^ mask, i) for i in range(devices)])


def vmem_call(kernel, out_shape, scratch, flops, smem=()):
    def call(*operands):
        specs = [
            pl.BlockSpec(memory_space=pltpu.SMEM if i in smem else pltpu.VMEM)
            for i in range(len(operands))
        ]
        outs = jax.tree.map(lambda _: pl.BlockSpec(memory_space=pltpu.VMEM), out_shape)
        return pl.pallas_call(
            kernel,
            out_shape=out_shape,
            in_specs=specs,
            out_specs=outs,
            scratch_shapes=scratch,
            compiler_params=pltpu.CompilerParams(vmem_limit_bytes=16 * 1024 * 1024),
            cost_estimate=pl.CostEstimate(
                flops=flops, bytes_accessed=1 << 20, transcendentals=0
            ),
        )(*operands)

    return call


def moved(field, distance):
    rows = field.shape[0]
    return pltpu.roll(field, distance % rows, 0) if distance % rows else field


def ahead_of(field, stride, side):
    row = lax.broadcasted_iota(jnp.int32, field.shape, 0)
    last = (row // stride) % side == side - 1
    return jnp.where(last, moved(field, (side - 1) * stride), moved(field, -stride))


def behind_of(field, stride, side):
    row = lax.broadcasted_iota(jnp.int32, field.shape, 0)
    start = (row // stride) % side == 0
    return jnp.where(start, moved(field, (1 - side) * stride), moved(field, stride))


def links_kernel(links_ref, out_ref, wide_ref, turned_ref):
    coefficients, cross, planes = links_ref.shape
    wide_ref[...] = links_ref[...].astype(F32)
    for at in range(cross):
        rows = pl.ds(at, planes, stride=cross)
        turned_ref[rows, :coefficients] = wide_ref[:, at, :].T
    out_ref[...] = turned_ref[...].astype(BF16)


def link_at(links, direction, colour, other):
    at = direction * 18 + colour * 3 + other
    return links[:, at : at + 1], links[:, at + 9 : at + 10]


def added(total, term):
    return term if total is None else total + term


def times_links(links, direction, vectors):
    parts = [None] * 6
    for colour in range(3):
        for other in range(3):
            real, imag = link_at(links, direction, colour, other)
            real_part, imag_part = vectors[other], vectors[3 + other]
            parts[colour] = added(parts[colour], real * real_part - imag * imag_part)
            parts[3 + colour] = added(parts[3 + colour], real * imag_part + imag * real_part)
    return parts


def times_adjoint(links, direction, vectors):
    parts = [None] * 6
    for colour in range(3):
        for other in range(3):
            real, imag = link_at(links, direction, colour, other)
            real_part, imag_part = vectors[colour], vectors[3 + colour]
            parts[other] = added(parts[other], real * real_part + imag * imag_part)
            parts[3 + other] = added(parts[3 + other], real * imag_part - imag * real_part)
    return [part.astype(BF16) for part in parts]


def across_slab(links, direction, vectors, side):
    stride = side**direction
    forward = times_links(links, direction, [ahead_of(v, stride, side) for v in vectors])
    adjoint = times_adjoint(links, direction, vectors)
    return [
        (part - behind_of(back.astype(F32), stride, side)).astype(BF16)
        for part, back in zip(forward, adjoint)
    ]


def slab_fields(ref):
    cells = ref.shape[0] // 6
    return [ref[k * cells : (k + 1) * cells, :].astype(F32) for k in range(6)]


def slab_kernel(side, vectors_ref, links_ref, copy_ref, out_ref):
    vectors = slab_fields(vectors_ref)
    links = links_ref[...].astype(F32)
    cells = links.shape[0]
    copy_ref[...] = vectors_ref[...]
    parts = across_slab(links, 0, vectors, side) + across_slab(links, 1, vectors, side)
    parts += times_adjoint(links, 2, vectors)
    for at, part in enumerate(parts):
        out_ref[at * cells : (at + 1) * cells, :] = part


def elementals_kernel(side, scale, slabs, early_ref, *refs):
    vector_refs, link_refs, out_refs = refs[:slabs], refs[slabs : 2 * slabs], refs[2 * slabs :]
    elem_ref, rhs_ref = out_refs
    modes = elem_ref.shape[-1]
    cells = link_refs[0].shape[0]
    sites = slabs * cells

    def put(slab, direction, parts):
        left, right = 2 * direction * modes, (2 * direction + 1) * modes
        for colour in range(3):
            low = colour * sites + slab * cells
            high = low + 3 * sites
            real_part, imag_part = parts[colour], parts[3 + colour]
            rhs_ref[low : low + cells, left : left + modes] = real_part
            rhs_ref[high : high + cells, left : left + modes] = imag_part
            rhs_ref[low : low + cells, right : right + modes] = imag_part
            rhs_ref[high : high + cells, right : right + modes] = -real_part

    early = [early_ref[at * cells : (at + 1) * cells, :] for at in range(18)]
    put(0, 0, early[:6])
    put(0, 1, early[6:12])
    vectors = [slab_fields(ref) for ref in vector_refs]
    links = [ref[...].astype(F32) for ref in link_refs]
    adjoint = [early[12:]]
    for slab in range(1, slabs):
        put(slab, 0, across_slab(links[slab], 0, vectors[slab], side))
        put(slab, 1, across_slab(links[slab], 1, vectors[slab], side))
        adjoint.append(times_adjoint(links[slab], 2, vectors[slab]))
    plane = side * side
    for slab in range(slabs):
        after, before = (slab + 1) % slabs, (slab - 1) % slabs
        ahead = [
            jnp.concatenate([here[plane:], there[:plane]], axis=0)
            for here, there in zip(vectors[slab], vectors[after])
        ]
        forward = times_links(links[slab], 2, ahead)
        parts = []
        for k in range(6):
            here, there = adjoint[slab][k].astype(F32), adjoint[before][k].astype(F32)
            behind = jnp.concatenate([there[cells - plane :], here[: cells - plane]], axis=0)
            parts.append((forward[k] - behind).astype(BF16))
        put(slab, 2, parts)

    fields = [ref[k * cells : (k + 1) * cells, :] for k in range(6) for ref in vector_refs]
    vectors = jnp.concatenate(fields, axis=0)
    product = lax.dot_general(
        vectors, rhs_ref[...], (((0,), (0,)), ((), ())), preferred_element_type=F32
    )
    for direction in range(3):
        left = 2 * direction * modes
        real_part = product[:, left : left + modes] * scale
        imag_part = product[:, left + modes : left + 2 * modes] * scale
        elem_ref[direction, 0] = real_part
        elem_ref[direction, 1] = imag_part


def operator_kernel(
    dirs_ref, elem_ref, rows_ref, oper_ref, first_ref, wide_ref, copy_ref
):
    modes = elem_ref.shape[-1]
    copy_ref[...] = rows_ref[...]
    picked = []
    for k in range(3):
        for part in range(2):
            picked.append(elem_ref[dirs_ref[k], part].astype(BF16).astype(F32))
    zero_real, zero_imag, one_real, one_imag, two_real, two_imag = picked
    sum_real = [[two_real, zero_real + one_imag], [zero_real - one_imag, -two_real]]
    sum_imag = [[two_imag, zero_imag - one_real], [zero_imag + one_real, -two_imag]]
    for p in range(2):
        for q in range(2):
            top, bottom = p * modes, (2 + p) * modes
            left, right = q * modes, (2 + q) * modes
            real_part = sum_real[p][q].astype(BF16)
            imag_part = sum_imag[p][q].astype(BF16)
            oper_ref[top : top + modes, left : left + modes] = -imag_part
            oper_ref[top : top + modes, right : right + modes] = real_part
            oper_ref[bottom : bottom + modes, left : left + modes] = -real_part
            oper_ref[bottom : bottom + modes, right : right + modes] = -imag_part
    product = times_operator(rows_ref[...], oper_ref[...])
    first_ref[...] = product.astype(BF16)
    wide_ref[...] = product


def times_operator(rows, operator):
    half = rows.shape[1] // 4
    upper = jnp.concatenate([rows[:, half : 2 * half], rows[:, 3 * half :]], axis=1)
    lower = jnp.concatenate([rows[:, :half], rows[:, 2 * half : 3 * half]], axis=1)
    both = jnp.dot(
        jnp.concatenate([upper, lower], axis=0), operator, preferred_element_type=F32
    )
    scale = 1.0 / math.sqrt(2.0 * half)
    count = rows.shape[0]
    above = both[:count] * scale
    below = both[count:] * (-scale)
    return jnp.concatenate([above[:, :half], below[:, :half], above[:, half:], below[:, half:]], 1)


def times_rows(left, right):
    order = left.shape[1] // 2
    count = left.shape[0]
    both = jnp.dot(
        jnp.concatenate([left[:, :order], left[:, order:]], axis=0),
        right,
        preferred_element_type=F32,
    )
    real_part = both[:count, :order] - both[count:, order:]
    imag_part = both[:count, order:] + both[count:, :order]
    return real_part, imag_part


def diagonal_sum(part, first_row):
    row = lax.broadcasted_iota(jnp.int32, part.shape, 0) + first_row
    column = lax.broadcasted_iota(jnp.int32, part.shape, 1)
    kept = jnp.where(row == column, part, 0.0)
    return jnp.sum(jnp.sum(kept, axis=0, keepdims=True), axis=1, keepdims=True)


def at_lanes(shape, values):
    lane = lax.broadcasted_iota(jnp.int32, shape, 1)
    total = jnp.zeros(shape, F32)
    for at, value in values:
        total = total + jnp.where(lane == at, value, 0.0)
    return total


def own_block(spaces, spins, space_step, spin_step):
    place = lax.rem(lax.axis_index("space") + space_step, spaces)
    spin = lax.rem(lax.axis_index("spin") + spin_step, spins)
    return place * spins + spin


def first_kernel(spaces, spins, oper_ref, own_ref, *refs):
    block_refs, first_ref = refs[:-1], refs[-1]
    count = own_ref.shape[0]
    start = pl.multiple_of(own_block(spaces, spins, 0, 0) * count, count)
    first_ref[pl.ds(start, count), :] = own_ref[...]
    at = 1
    left = list(block_refs)
    while left:
        rows = left.pop(0)[...]
        while rows.shape[0] < count:
            rows = jnp.concatenate([rows, left.pop(0)[...]], axis=0)
        product = times_operator(rows, oper_ref[...])
        start = pl.multiple_of(own_block(spaces, spins, at // spins, at % spins) * count, count)
        first_ref[pl.ds(start, count), :] = product.astype(BF16)
        at += 1


def second_kernel(next_ref, first_ref, second_ref, wide_ref):
    order = next_ref.shape[1] // 2
    real_part, imag_part = times_rows(next_ref[...], first_ref[...])
    second_ref[:, :order] = real_part.astype(BF16)
    second_ref[:, order:] = imag_part.astype(BF16)
    wide_ref[:, :order] = real_part
    wide_ref[:, order:] = imag_part


def turn_kernel(spaces, spins, offsets_ref, times_ref, first_ref, elem_ref, *refs):
    one_ref, two_ref, out_ref, weights_ref, share_ref, trace_ref, wide_ref = refs
    count, width = out_ref.shape
    order, lanes = width // 2, wide_ref.shape[0]
    first_row = own_block(spaces, spins, 0, 0) * count
    start = pl.multiple_of(first_row // lanes * lanes, lanes)
    for part in range(2):
        block = first_ref[:, pl.ds(pl.multiple_of(start + part * order, lanes), lanes)]
        wide_ref[:, part * order : (part + 1) * order] = block.astype(F32).T
    rows = pl.ds(pl.multiple_of(first_row - start, count), count)
    out_ref[...] = wide_ref[rows, :].astype(BF16)
    values = []
    for at, part_ref in enumerate((one_ref, two_ref)):
        values.append((2 * at, diagonal_sum(part_ref[:, :order], first_row)))
        values.append((2 * at + 1, diagonal_sum(part_ref[:, order:], first_row)))
    trace_ref[...] = at_lanes(trace_ref.shape, values)
    lane = lax.broadcasted_iota(jnp.int32, weights_ref.shape, 1)
    row = lax.broadcasted_iota(jnp.int32, weights_ref.shape, 0)
    counts = jnp.zeros(weights_ref.shape, F32)
    for j in range(offsets_ref.shape[0]):
        counts = counts + jnp.where(lane // 2 == offsets_ref[j], 1.0, 0.0)
    counts = jnp.where((lane < 6) & (lane % 2 == row), counts, 0.0)
    weights_ref[...] = counts
    here = jnp.where(times_ref[...] == lax.axis_index("tm"), 1.0, 0.0)
    weights_ref[2:3, : here.shape[1]] = here
    rows, columns = share_ref.shape[0], share_ref.shape[3]
    modes = elem_ref.shape[3]
    top = pl.multiple_of(lax.axis_index("space") * rows, rows)
    turn = lax.rem(modes - lax.axis_index("spin") * columns, modes)
    for direction in range(3):
        for part in range(2):
            block = elem_ref[direction, part, pl.ds(top, rows), :]
            share_ref[:, direction, part, :] = pltpu.roll(block, turn, 1)[:, :columns]


def whole_sum(values):
    return jnp.sum(jnp.sum(values, axis=0, keepdims=True), axis=1, keepdims=True)


def share_kernel(weights_ref, second_ref, turned_ref, early_ref, out_ref):
    order = second_ref.shape[1] // 2
    left_real, left_imag = second_ref[:, :order].astype(F32), second_ref[:, order:].astype(F32)
    right_real, right_imag = turned_ref[:, :order].astype(F32), turned_ref[:, order:].astype(F32)
    real_part = whole_sum(left_real * right_real - left_imag * right_imag)
    imag_part = whole_sum(left_real * right_imag + left_imag * right_real)
    traces = early_ref[0:1, :] + at_lanes((1, 128), [(4, real_part), (5, imag_part)])
    values = jnp.sum(traces * weights_ref[0:2, :], axis=1, keepdims=True)
    out_ref[...] = values * weights_ref[2:3, : out_ref.shape[1]]


def third_kernel(second_ref, first_ref, chain_ref):
    order = second_ref.shape[1] // 2
    real_part, imag_part = times_rows(second_ref[...], first_ref[...])
    scale = math.sqrt(order)
    chain_ref[:, :order] = (real_part * scale).astype(BF16)
    chain_ref[:, order:] = (imag_part * scale).astype(BF16)


def on_device(
    eigenvectors, gauge_links, perambulators, source_times, insert_offsets, derivative_dirs
):
    spaces, spins, slots = lax.axis_size("space"), lax.axis_size("spin"), lax.axis_size("tm")
    planes, side, modes = eigenvectors.shape[3], eigenvectors.shape[4], eigenvectors.shape[6]
    cells = planes * side * side
    own_rows = perambulators[0]
    count, width = own_rows.shape
    order = width // 2

    field = eigenvectors.reshape((6 * cells, modes))
    fields = [field] + [from_offset(field, "space", step) for step in range(1, spaces)]
    link = jnp.swapaxes(gauge_links.reshape((54, planes, side * side)), 1, 2)
    link = vmem_call(
        links_kernel,
        jax.ShapeDtypeStruct((cells, modes), BF16),
        [pltpu.VMEM(link.shape, F32), pltpu.VMEM((cells, modes), F32)],
        10**6,
    )(link)
    links = [link] + [from_offset(link, "space", step) for step in range(1, spaces)]
    fields[0], own_slab = vmem_call(
        functools.partial(slab_kernel, side),
        (
            jax.ShapeDtypeStruct(field.shape, BF16),
            jax.ShapeDtypeStruct((18 * cells, modes), BF16),
        ),
        [],
        10**6,
    )(field, link)

    held_rows, own_slab = lax.optimization_barrier((own_rows, own_slab))
    far_rows = [from_offset(held_rows, "space", step) for step in range(1, spaces)]

    norm_scale = 1.0 / math.sqrt(6.0 * 4.0 * planes * spaces * side * side)
    rows_shape = jax.ShapeDtypeStruct((count, width), BF16)
    trace_shape = jax.ShapeDtypeStruct((8, 128), F32)
    elements = vmem_call(
        functools.partial(elementals_kernel, side, norm_scale, spaces),
        jax.ShapeDtypeStruct((3, 2, modes, modes), F32),
        [pltpu.VMEM((6 * cells * spaces, 6 * modes), BF16)],
        10**10,
    )(own_slab, *fields, *links)
    wide_shape = jax.ShapeDtypeStruct((count, width), F32)
    operator, own_first, own_wide, rows_copy = vmem_call(
        operator_kernel,
        (jax.ShapeDtypeStruct((4 * modes, 4 * modes), BF16), rows_shape, wide_shape, rows_shape),
        [],
        10**8,
        smem=(0,),
    )(derivative_dirs, elements, own_rows)

    next_first = from_offset(own_first, "tm", 1)

    far_rows, held_rows, held_first = lax.optimization_barrier((far_rows, rows_copy, own_first))
    blocks = []
    for at, block in enumerate([held_rows] + far_rows):
        blocks += [block]
        pieces = PIECES if at else 1
        for step in range(1, spins):
            for piece in range(pieces):
                low, high = piece * count // pieces, (piece + 1) * count // pieces
                blocks += [from_offset(block[low:high], "spin", step)]
    blocks = blocks[1:]
    first = vmem_call(
        functools.partial(first_kernel, spaces, spins),
        jax.ShapeDtypeStruct((order, width), BF16),
        [],
        10**6,
    )(operator, held_first, *blocks)

    second, second_wide = vmem_call(
        second_kernel,
        (rows_shape, wide_shape),
        [],
        3 * 10**8,
    )(next_first, first)

    next_second = from_offset(second, "tm", 1)

    turned, weights, elementals, early = vmem_call(
        functools.partial(turn_kernel, spaces, spins),
        (
            rows_shape,
            trace_shape,
            jax.ShapeDtypeStruct((modes // spaces, 3, 2, modes // spins), F32),
            trace_shape,
        ),
        [pltpu.VMEM((max(count, 128), width), F32)],
        10**6,
        smem=(0,),
    )(insert_offsets, source_times[None, :], first, elements, own_wide, second_wide)
    shares = vmem_call(
        share_kernel,
        jax.ShapeDtypeStruct((2, source_times.shape[0]), F32),
        [],
        10**6,
    )(weights, next_second, turned, early)
    chain = vmem_call(third_kernel, rows_shape, [], 10**8)(next_second, first)

    devices = slots * spaces * spins
    if devices & (devices - 1):
        shares = lax.psum(shares, ("tm", "space", "spin"))
    else:
        bits = [1 << at for at in range(devices.bit_length() - 1)]
        while bits:
            low, high = bits[0], bits[-1]
            bits = bits[1:-1]
            masks = [low] if low == high else [low, high, low | high]
            parts = [swapped(shares, devices, mask) for mask in masks]
            shares = functools.reduce(lambda x, y: x + y, parts, shares)
    return (elementals[None], chain[None], shares.T)


def solution(mesh):
    in_specs = (
        P(("cfg", "tm"), None, None, "space", None, None, None),
        P(("cfg", "tm"), None, None, None, None, "space", None),
        P(("cfg", "tm"), ("space", "spin"), None),
        P(),
        P(),
        P(),
    )
    out_specs = (
        P(("cfg", "tm"), "space", None, None, "spin"),
        P(("cfg", "tm"), ("space", "spin"), None),
        P("cfg", None),
    )
    return jax.shard_map(
        on_device, mesh=mesh, in_specs=in_specs, out_specs=out_specs, check_vma=False
    )
```

```python
import functools
import math

import jax
import jax.numpy as jnp
from jax import lax
from jax.experimental import pallas as pl
from jax.experimental.pallas import tpu as pltpu

from jax.sharding import PartitionSpec as P

F32 = jnp.float32
BF16 = jnp.bfloat16
PIECES = 2


def from_offset(block, axis, distance):
    count = lax.axis_size(axis)
    return lax.ppermute(block, axis, [((i + distance) % count, i) for i in range(count)])


def swapped(block, devices, mask):
    return lax.ppermute(block, ("tm", "space", "spin"), [(i ^ mask, i) for i in range(devices)])


def vmem_call(kernel, out_shape, scratch, flops, smem=()):
    def call(*operands):
        specs = [
            pl.BlockSpec(memory_space=pltpu.SMEM if i in smem else pltpu.VMEM)
            for i in range(len(operands))
        ]
        outs = jax.tree.map(lambda _: pl.BlockSpec(memory_space=pltpu.VMEM), out_shape)
        return pl.pallas_call(
            kernel,
            out_shape=out_shape,
            in_specs=specs,
            out_specs=outs,
            scratch_shapes=scratch,
            compiler_params=pltpu.CompilerParams(vmem_limit_bytes=16 * 1024 * 1024),
            cost_estimate=pl.CostEstimate(
                flops=flops, bytes_accessed=1 << 20, transcendentals=0
            ),
        )(*operands)

    return call


def moved(field, distance):
    rows = field.shape[0]
    return pltpu.roll(field, distance % rows, 0) if distance % rows else field


def ahead_of(field, stride, side):
    row = lax.broadcasted_iota(jnp.int32, field.shape, 0)
    last = (row // stride) % side == side - 1
    return jnp.where(last, moved(field, (side - 1) * stride), moved(field, -stride))


def behind_of(field, stride, side):
    row = lax.broadcasted_iota(jnp.int32, field.shape, 0)
    start = (row // stride) % side == 0
    return jnp.where(start, moved(field, (1 - side) * stride), moved(field, stride))


def links_kernel(links_ref, out_ref, wide_ref, turned_ref):
    coefficients, cross, planes = links_ref.shape
    wide_ref[...] = links_ref[...].astype(F32)
    for at in range(cross):
        rows = pl.ds(at, planes, stride=cross)
        turned_ref[rows, :coefficients] = wide_ref[:, at, :].T
    out_ref[...] = turned_ref[...].astype(BF16)


def link_at(links, direction, colour, other):
    at = direction * 18 + colour * 3 + other
    return links[:, at : at + 1], links[:, at + 9 : at + 10]


def added(total, term):
    return term if total is None else total + term


def times_links(links, direction, vectors):
    parts = [None] * 6
    for colour in range(3):
        for other in range(3):
            real, imag = link_at(links, direction, colour, other)
            real_part, imag_part = vectors[other], vectors[3 + other]
            parts[colour] = added(parts[colour], real * real_part - imag * imag_part)
            parts[3 + colour] = added(parts[3 + colour], real * imag_part + imag * real_part)
    return parts


def times_adjoint(links, direction, vectors):
    parts = [None] * 6
    for colour in range(3):
        for other in range(3):
            real, imag = link_at(links, direction, colour, other)
            real_part, imag_part = vectors[colour], vectors[3 + colour]
            parts[other] = added(parts[other], real * real_part + imag * imag_part)
            parts[3 + other] = added(parts[3 + other], real * imag_part - imag * real_part)
    return [part.astype(BF16) for part in parts]


def across_slab(links, direction, vectors, side):
    stride = side**direction
    forward = times_links(links, direction, [ahead_of(v, stride, side) for v in vectors])
    adjoint = times_adjoint(links, direction, vectors)
    return [
        (part - behind_of(back.astype(F32), stride, side)).astype(BF16)
        for part, back in zip(forward, adjoint)
    ]


def slab_fields(ref):
    cells = ref.shape[0] // 6
    return [ref[k * cells : (k + 1) * cells, :].astype(F32) for k in range(6)]


def slab_kernel(side, vectors_ref, links_ref, copy_ref, out_ref):
    vectors = slab_fields(vectors_ref)
    links = links_ref[...].astype(F32)
    cells = links.shape[0]
    copy_ref[...] = vectors_ref[...]
    parts = across_slab(links, 0, vectors, side) + across_slab(links, 1, vectors, side)
    parts += times_adjoint(links, 2, vectors)
    for at, part in enumerate(parts):
        out_ref[at * cells : (at + 1) * cells, :] = part


def elementals_kernel(side, scale, slabs, early_ref, *refs):
    vector_refs, link_refs, out_refs = refs[:slabs], refs[slabs : 2 * slabs], refs[2 * slabs :]
    elem_ref, rhs_ref = out_refs
    modes = elem_ref.shape[-1]
    cells = link_refs[0].shape[0]
    sites = slabs * cells

    def put(slab, direction, parts):
        left, right = 2 * direction * modes, (2 * direction + 1) * modes
        for colour in range(3):
            low = colour * sites + slab * cells
            high = low + 3 * sites
            real_part, imag_part = parts[colour], parts[3 + colour]
            rhs_ref[low : low + cells, left : left + modes] = real_part
            rhs_ref[high : high + cells, left : left + modes] = imag_part
            rhs_ref[low : low + cells, right : right + modes] = imag_part
            rhs_ref[high : high + cells, right : right + modes] = -real_part

    early = [early_ref[at * cells : (at + 1) * cells, :] for at in range(18)]
    put(0, 0, early[:6])
    put(0, 1, early[6:12])
    vectors = [slab_fields(ref) for ref in vector_refs]
    links = [ref[...].astype(F32) for ref in link_refs]
    adjoint = [early[12:]]
    for slab in range(1, slabs):
        put(slab, 0, across_slab(links[slab], 0, vectors[slab], side))
        put(slab, 1, across_slab(links[slab], 1, vectors[slab], side))
        adjoint.append(times_adjoint(links[slab], 2, vectors[slab]))
    plane = side * side
    for slab in range(slabs):
        after, before = (slab + 1) % slabs, (slab - 1) % slabs
        ahead = [
            jnp.concatenate([here[plane:], there[:plane]], axis=0)
            for here, there in zip(vectors[slab], vectors[after])
        ]
        forward = times_links(links[slab], 2, ahead)
        parts = []
        for k in range(6):
            here, there = adjoint[slab][k].astype(F32), adjoint[before][k].astype(F32)
            behind = jnp.concatenate([there[cells - plane :], here[: cells - plane]], axis=0)
            parts.append((forward[k] - behind).astype(BF16))
        put(slab, 2, parts)

    fields = [ref[k * cells : (k + 1) * cells, :] for k in range(6) for ref in vector_refs]
    vectors = jnp.concatenate(fields, axis=0)
    product = lax.dot_general(
        vectors, rhs_ref[...], (((0,), (0,)), ((), ())), preferred_element_type=F32
    )
    for direction in range(3):
        left = 2 * direction * modes
        real_part = product[:, left : left + modes] * scale
        imag_part = product[:, left + modes : left + 2 * modes] * scale
        elem_ref[direction, 0] = real_part
        elem_ref[direction, 1] = imag_part


def operator_kernel(
    dirs_ref, elem_ref, rows_ref, oper_ref, first_ref, wide_ref, copy_ref
):
    modes = elem_ref.shape[-1]
    copy_ref[...] = rows_ref[...]
    picked = []
    for k in range(3):
        for part in range(2):
            picked.append(elem_ref[dirs_ref[k], part].astype(BF16).astype(F32))
    zero_real, zero_imag, one_real, one_imag, two_real, two_imag = picked
    sum_real = [[two_real, zero_real + one_imag], [zero_real - one_imag, -two_real]]
    sum_imag = [[two_imag, zero_imag - one_real], [zero_imag + one_real, -two_imag]]
    for p in range(2):
        for q in range(2):
            top, bottom = p * modes, (2 + p) * modes
            left, right = q * modes, (2 + q) * modes
            real_part = sum_real[p][q].astype(BF16)
            imag_part = sum_imag[p][q].astype(BF16)
            oper_ref[top : top + modes, left : left + modes] = -imag_part
            oper_ref[top : top + modes, right : right + modes] = real_part
            oper_ref[bottom : bottom + modes, left : left + modes] = -real_part
            oper_ref[bottom : bottom + modes, right : right + modes] = -imag_part
    product = times_operator(rows_ref[...], oper_ref[...])
    first_ref[...] = product.astype(BF16)
    wide_ref[...] = product


def times_operator(rows, operator):
    half = rows.shape[1] // 4
    upper = jnp.concatenate([rows[:, half : 2 * half], rows[:, 3 * half :]], axis=1)
    lower = jnp.concatenate([rows[:, :half], rows[:, 2 * half : 3 * half]], axis=1)
    both = jnp.dot(
        jnp.concatenate([upper, lower], axis=0), operator, preferred_element_type=F32
    )
    scale = 1.0 / math.sqrt(2.0 * half)
    count = rows.shape[0]
    above = both[:count] * scale
    below = both[count:] * (-scale)
    return jnp.concatenate([above[:, :half], below[:, :half], above[:, half:], below[:, half:]], 1)


def times_rows(left, right):
    order = left.shape[1] // 2
    count = left.shape[0]
    both = jnp.dot(
        jnp.concatenate([left[:, :order], left[:, order:]], axis=0),
        right,
        preferred_element_type=F32,
    )
    real_part = both[:count, :order] - both[count:, order:]
    imag_part = both[:count, order:] + both[count:, :order]
    return real_part, imag_part


def diagonal_sum(part, first_row):
    row = lax.broadcasted_iota(jnp.int32, part.shape, 0) + first_row
    column = lax.broadcasted_iota(jnp.int32, part.shape, 1)
    kept = jnp.where(row == column, part, 0.0)
    return jnp.sum(jnp.sum(kept, axis=0, keepdims=True), axis=1, keepdims=True)


def at_lanes(shape, values):
    lane = lax.broadcasted_iota(jnp.int32, shape, 1)
    total = jnp.zeros(shape, F32)
    for at, value in values:
        total = total + jnp.where(lane == at, value, 0.0)
    return total


def own_block(spaces, spins, space_step, spin_step):
    place = lax.rem(lax.axis_index("space") + space_step, spaces)
    spin = lax.rem(lax.axis_index("spin") + spin_step, spins)
    return place * spins + spin


def first_kernel(spaces, spins, oper_ref, own_ref, *refs):
    block_refs, first_ref = refs[:-1], refs[-1]
    count = own_ref.shape[0]
    start = pl.multiple_of(own_block(spaces, spins, 0, 0) * count, count)
    first_ref[pl.ds(start, count), :] = own_ref[...]
    at = 1
    left = list(block_refs)
    while left:
        rows = left.pop(0)[...]
        while rows.shape[0] < count:
            rows = jnp.concatenate([rows, left.pop(0)[...]], axis=0)
        product = times_operator(rows, oper_ref[...])
        start = pl.multiple_of(own_block(spaces, spins, at // spins, at % spins) * count, count)
        first_ref[pl.ds(start, count), :] = product.astype(BF16)
        at += 1


def second_kernel(next_ref, first_ref, second_ref, wide_ref):
    order = next_ref.shape[1] // 2
    real_part, imag_part = times_rows(next_ref[...], first_ref[...])
    second_ref[:, :order] = real_part.astype(BF16)
    second_ref[:, order:] = imag_part.astype(BF16)
    wide_ref[:, :order] = real_part
    wide_ref[:, order:] = imag_part


def turn_kernel(spaces, spins, offsets_ref, times_ref, first_ref, elem_ref, *refs):
    one_ref, two_ref, out_ref, weights_ref, share_ref, trace_ref, wide_ref = refs
    count, width = out_ref.shape
    order, lanes = width // 2, wide_ref.shape[0]
    first_row = own_block(spaces, spins, 0, 0) * count
    start = pl.multiple_of(first_row // lanes * lanes, lanes)
    for part in range(2):
        block = first_ref[:, pl.ds(pl.multiple_of(start + part * order, lanes), lanes)]
        wide_ref[:, part * order : (part + 1) * order] = block.astype(F32).T
    rows = pl.ds(pl.multiple_of(first_row - start, count), count)
    out_ref[...] = wide_ref[rows, :].astype(BF16)
    values = []
    for at, part_ref in enumerate((one_ref, two_ref)):
        values.append((2 * at, diagonal_sum(part_ref[:, :order], first_row)))
        values.append((2 * at + 1, diagonal_sum(part_ref[:, order:], first_row)))
    trace_ref[...] = at_lanes(trace_ref.shape, values)
    lane = lax.broadcasted_iota(jnp.int32, weights_ref.shape, 1)
    row = lax.broadcasted_iota(jnp.int32, weights_ref.shape, 0)
    counts = jnp.zeros(weights_ref.shape, F32)
    for j in range(offsets_ref.shape[0]):
        counts = counts + jnp.where(lane // 2 == offsets_ref[j], 1.0, 0.0)
    counts = jnp.where((lane < 6) & (lane % 2 == row), counts, 0.0)
    weights_ref[...] = counts
    here = jnp.where(times_ref[...] == lax.axis_index("tm"), 1.0, 0.0)
    weights_ref[2:3, : here.shape[1]] = here
    rows, columns = share_ref.shape[0], share_ref.shape[3]
    modes = elem_ref.shape[3]
    top = pl.multiple_of(lax.axis_index("space") * rows, rows)
    turn = lax.rem(modes - lax.axis_index("spin") * columns, modes)
    for direction in range(3):
        for part in range(2):
            block = elem_ref[direction, part, pl.ds(top, rows), :]
            share_ref[:, direction, part, :] = pltpu.roll(block, turn, 1)[:, :columns]


def whole_sum(values):
    return jnp.sum(jnp.sum(values, axis=0, keepdims=True), axis=1, keepdims=True)


def share_kernel(weights_ref, second_ref, turned_ref, early_ref, out_ref):
    order = second_ref.shape[1] // 2
    left_real, left_imag = second_ref[:, :order].astype(F32), second_ref[:, order:].astype(F32)
    right_real, right_imag = turned_ref[:, :order].astype(F32), turned_ref[:, order:].astype(F32)
    real_part = whole_sum(left_real * right_real - left_imag * right_imag)
    imag_part = whole_sum(left_real * right_imag + left_imag * right_real)
    traces = early_ref[0:1, :] + at_lanes((1, 128), [(4, real_part), (5, imag_part)])
    values = jnp.sum(traces * weights_ref[0:2, :], axis=1, keepdims=True)
    out_ref[...] = values * weights_ref[2:3, : out_ref.shape[1]]


def third_kernel(second_ref, first_ref, chain_ref):
    order = second_ref.shape[1] // 2
    real_part, imag_part = times_rows(second_ref[...], first_ref[...])
    scale = math.sqrt(order)
    chain_ref[:, :order] = (real_part * scale).astype(BF16)
    chain_ref[:, order:] = (imag_part * scale).astype(BF16)


def on_device(
    eigenvectors, gauge_links, perambulators, source_times, insert_offsets, derivative_dirs
):
    spaces, spins, slots = lax.axis_size("space"), lax.axis_size("spin"), lax.axis_size("tm")
    planes, side, modes = eigenvectors.shape[3], eigenvectors.shape[4], eigenvectors.shape[6]
    cells = planes * side * side
    own_rows = perambulators[0]
    count, width = own_rows.shape
    order = width // 2

    field = eigenvectors.reshape((6 * cells, modes))
    fields = [field] + [from_offset(field, "space", step) for step in range(1, spaces)]
    link = jnp.swapaxes(gauge_links.reshape((54, planes, side * side)), 1, 2)
    link = vmem_call(
        links_kernel,
        jax.ShapeDtypeStruct((cells, modes), BF16),
        [pltpu.VMEM(link.shape, F32), pltpu.VMEM((cells, modes), F32)],
        10**9,
    )(link)
    links = [link] + [from_offset(link, "space", step) for step in range(1, spaces)]
    fields[0], own_slab = vmem_call(
        functools.partial(slab_kernel, side),
        (
            jax.ShapeDtypeStruct(field.shape, BF16),
            jax.ShapeDtypeStruct((18 * cells, modes), BF16),
        ),
        [],
        10**6,
    )(field, link)

    held_rows, own_slab = lax.optimization_barrier((own_rows, own_slab))
    far_rows = [from_offset(held_rows, "space", step) for step in range(1, spaces)]

    norm_scale = 1.0 / math.sqrt(6.0 * 4.0 * planes * spaces * side * side)
    rows_shape = jax.ShapeDtypeStruct((count, width), BF16)
    trace_shape = jax.ShapeDtypeStruct((8, 128), F32)
    elements = vmem_call(
        functools.partial(elementals_kernel, side, norm_scale, spaces),
        jax.ShapeDtypeStruct((3, 2, modes, modes), F32),
        [pltpu.VMEM((6 * cells * spaces, 6 * modes), BF16)],
        10**10,
    )(own_slab, *fields, *links)
    wide_shape = jax.ShapeDtypeStruct((count, width), F32)
    operator, own_first, own_wide, rows_copy = vmem_call(
        operator_kernel,
        (jax.ShapeDtypeStruct((4 * modes, 4 * modes), BF16), rows_shape, wide_shape, rows_shape),
        [],
        10**8,
        smem=(0,),
    )(derivative_dirs, elements, own_rows)

    next_first = from_offset(own_first, "tm", 1)

    far_rows, held_rows, held_first = lax.optimization_barrier((far_rows, rows_copy, own_first))
    blocks = []
    for at, block in enumerate([held_rows] + far_rows):
        blocks += [block]
        pieces = PIECES if at else 1
        for step in range(1, spins):
            for piece in range(pieces):
                low, high = piece * count // pieces, (piece + 1) * count // pieces
                blocks += [from_offset(block[low:high], "spin", step)]
    blocks = blocks[1:]
    first = vmem_call(
        functools.partial(first_kernel, spaces, spins),
        jax.ShapeDtypeStruct((order, width), BF16),
        [],
        10**6,
    )(operator, held_first, *blocks)

    second, second_wide = vmem_call(
        second_kernel,
        (rows_shape, wide_shape),
        [],
        3 * 10**8,
    )(next_first, first)

    next_second = from_offset(second, "tm", 1)

    turned, weights, elementals, early = vmem_call(
        functools.partial(turn_kernel, spaces, spins),
        (
            rows_shape,
            trace_shape,
            jax.ShapeDtypeStruct((modes // spaces, 3, 2, modes // spins), F32),
            trace_shape,
        ),
        [pltpu.VMEM((max(count, 128), width), F32)],
        10**6,
        smem=(0,),
    )(insert_offsets, source_times[None, :], first, elements, own_wide, second_wide)
    shares = vmem_call(
        share_kernel,
        jax.ShapeDtypeStruct((2, source_times.shape[0]), F32),
        [],
        10**6,
    )(weights, next_second, turned, early)
    chain = vmem_call(third_kernel, rows_shape, [], 10**8)(next_second, first)

    devices = slots * spaces * spins
    if devices & (devices - 1):
        shares = lax.psum(shares, ("tm", "space", "spin"))
    else:
        bits = [1 << at for at in range(devices.bit_length() - 1)]
        while bits:
            low, high = bits[0], bits[-1]
            bits = bits[1:-1]
            masks = [low] if low == high else [low, high, low | high]
            parts = [swapped(shares, devices, mask) for mask in masks]
            shares = functools.reduce(lambda x, y: x + y, parts, shares)
    return (elementals[None], chain[None], shares.T)


def solution(mesh):
    in_specs = (
        P(("cfg", "tm"), None, None, "space", None, None, None),
        P(("cfg", "tm"), None, None, None, None, "space", None),
        P(("cfg", "tm"), ("space", "spin"), None),
        P(),
        P(),
        P(),
    )
    out_specs = (
        P(("cfg", "tm"), "space", None, None, "spin"),
        P(("cfg", "tm"), ("space", "spin"), None),
        P("cfg", None),
    )
    return jax.shard_map(
        on_device, mesh=mesh, in_specs=in_specs, out_specs=out_specs, check_vma=False
    )
```

```python
import functools
import math

import jax
import jax.numpy as jnp
from jax import lax
from jax.experimental import pallas as pl
from jax.experimental.pallas import tpu as pltpu

from jax.sharding import PartitionSpec as P

F32 = jnp.float32
BF16 = jnp.bfloat16
PIECES = 2


def from_offset(block, axis, distance):
    count = lax.axis_size(axis)
    return lax.ppermute(block, axis, [((i + distance) % count, i) for i in range(count)])


def swapped(block, devices, mask):
    return lax.ppermute(block, ("tm", "space", "spin"), [(i ^ mask, i) for i in range(devices)])


def vmem_call(kernel, out_shape, scratch, flops, smem=()):
    def call(*operands):
        specs = [
            pl.BlockSpec(memory_space=pltpu.SMEM if i in smem else pltpu.VMEM)
            for i in range(len(operands))
        ]
        outs = jax.tree.map(lambda _: pl.BlockSpec(memory_space=pltpu.VMEM), out_shape)
        return pl.pallas_call(
            kernel,
            out_shape=out_shape,
            in_specs=specs,
            out_specs=outs,
            scratch_shapes=scratch,
            compiler_params=pltpu.CompilerParams(vmem_limit_bytes=16 * 1024 * 1024),
            cost_estimate=pl.CostEstimate(
                flops=flops, bytes_accessed=1 << 20, transcendentals=0
            ),
        )(*operands)

    return call


def moved(field, distance):
    rows = field.shape[0]
    return pltpu.roll(field, distance % rows, 0) if distance % rows else field


def ahead_of(field, stride, side):
    row = lax.broadcasted_iota(jnp.int32, field.shape, 0)
    last = (row // stride) % side == side - 1
    return jnp.where(last, moved(field, (side - 1) * stride), moved(field, -stride))


def behind_of(field, stride, side):
    row = lax.broadcasted_iota(jnp.int32, field.shape, 0)
    start = (row // stride) % side == 0
    return jnp.where(start, moved(field, (1 - side) * stride), moved(field, stride))


def links_kernel(links_ref, out_ref, wide_ref, turned_ref):
    coefficients, cross, planes = links_ref.shape
    wide_ref[...] = links_ref[...].astype(F32)
    for at in range(cross):
        rows = pl.ds(at, planes, stride=cross)
        turned_ref[rows, :coefficients] = wide_ref[:, at, :].T
    out_ref[...] = turned_ref[...].astype(BF16)


def link_at(links, direction, colour, other):
    at = direction * 18 + colour * 3 + other
    return links[:, at : at + 1], links[:, at + 9 : at + 10]


def added(total, term):
    return term if total is None else total + term


def times_links(links, direction, vectors):
    parts = [None] * 6
    for colour in range(3):
        for other in range(3):
            real, imag = link_at(links, direction, colour, other)
            real_part, imag_part = vectors[other], vectors[3 + other]
            parts[colour] = added(parts[colour], real * real_part - imag * imag_part)
            parts[3 + colour] = added(parts[3 + colour], real * imag_part + imag * real_part)
    return parts


def times_adjoint(links, direction, vectors):
    parts = [None] * 6
    for colour in range(3):
        for other in range(3):
            real, imag = link_at(links, direction, colour, other)
            real_part, imag_part = vectors[colour], vectors[3 + colour]
            parts[other] = added(parts[other], real * real_part + imag * imag_part)
            parts[3 + other] = added(parts[3 + other], real * imag_part - imag * real_part)
    return [part.astype(BF16) for part in parts]


def across_slab(links, direction, vectors, side):
    stride = side**direction
    forward = times_links(links, direction, [ahead_of(v, stride, side) for v in vectors])
    adjoint = times_adjoint(links, direction, vectors)
    return [
        (part - behind_of(back.astype(F32), stride, side)).astype(BF16)
        for part, back in zip(forward, adjoint)
    ]


def slab_fields(ref):
    cells = ref.shape[0] // 6
    return [ref[k * cells : (k + 1) * cells, :].astype(F32) for k in range(6)]


def slab_kernel(side, vectors_ref, links_ref, copy_ref, out_ref):
    vectors = slab_fields(vectors_ref)
    links = links_ref[...].astype(F32)
    cells = links.shape[0]
    copy_ref[...] = vectors_ref[...]
    parts = across_slab(links, 0, vectors, side) + across_slab(links, 1, vectors, side)
    parts += times_adjoint(links, 2, vectors)
    for at, part in enumerate(parts):
        out_ref[at * cells : (at + 1) * cells, :] = part


def elementals_kernel(side, scale, slabs, early_ref, *refs):
    vector_refs, link_refs, out_refs = refs[:slabs], refs[slabs : 2 * slabs], refs[2 * slabs :]
    elem_ref, rhs_ref = out_refs
    modes = elem_ref.shape[-1]
    cells = link_refs[0].shape[0]
    sites = slabs * cells

    def put(slab, direction, parts):
        left, right = 2 * direction * modes, (2 * direction + 1) * modes
        for colour in range(3):
            low = colour * sites + slab * cells
            high = low + 3 * sites
            real_part, imag_part = parts[colour], parts[3 + colour]
            rhs_ref[low : low + cells, left : left + modes] = real_part
            rhs_ref[high : high + cells, left : left + modes] = imag_part
            rhs_ref[low : low + cells, right : right + modes] = imag_part
            rhs_ref[high : high + cells, right : right + modes] = -real_part

    early = [early_ref[at * cells : (at + 1) * cells, :] for at in range(18)]
    put(0, 0, early[:6])
    put(0, 1, early[6:12])
    vectors = [slab_fields(ref) for ref in vector_refs]
    links = [ref[...].astype(F32) for ref in link_refs]
    adjoint = [early[12:]]
    for slab in range(1, slabs):
        put(slab, 0, across_slab(links[slab], 0, vectors[slab], side))
        put(slab, 1, across_slab(links[slab], 1, vectors[slab], side))
        adjoint.append(times_adjoint(links[slab], 2, vectors[slab]))
    plane = side * side
    for slab in range(slabs):
        after, before = (slab + 1) % slabs, (slab - 1) % slabs
        ahead = [
            jnp.concatenate([here[plane:], there[:plane]], axis=0)
            for here, there in zip(vectors[slab], vectors[after])
        ]
        forward = times_links(links[slab], 2, ahead)
        parts = []
        for k in range(6):
            here, there = adjoint[slab][k].astype(F32), adjoint[before][k].astype(F32)
            behind = jnp.concatenate([there[cells - plane :], here[: cells - plane]], axis=0)
            parts.append((forward[k] - behind).astype(BF16))
        put(slab, 2, parts)

    fields = [ref[k * cells : (k + 1) * cells, :] for k in range(6) for ref in vector_refs]
    vectors = jnp.concatenate(fields, axis=0)
    product = lax.dot_general(
        vectors, rhs_ref[...], (((0,), (0,)), ((), ())), preferred_element_type=F32
    )
    for direction in range(3):
        left = 2 * direction * modes
        real_part = product[:, left : left + modes] * scale
        imag_part = product[:, left + modes : left + 2 * modes] * scale
        elem_ref[direction, 0] = real_part
        elem_ref[direction, 1] = imag_part


def operator_kernel(
    dirs_ref, elem_ref, rows_ref, oper_ref, first_ref, wide_ref
):
    modes = elem_ref.shape[-1]
    picked = []
    for k in range(3):
        for part in range(2):
            picked.append(elem_ref[dirs_ref[k], part].astype(BF16).astype(F32))
    zero_real, zero_imag, one_real, one_imag, two_real, two_imag = picked
    sum_real = [[two_real, zero_real + one_imag], [zero_real - one_imag, -two_real]]
    sum_imag = [[two_imag, zero_imag - one_real], [zero_imag + one_real, -two_imag]]
    for p in range(2):
        for q in range(2):
            top, bottom = p * modes, (2 + p) * modes
            left, right = q * modes, (2 + q) * modes
            real_part = sum_real[p][q].astype(BF16)
            imag_part = sum_imag[p][q].astype(BF16)
            oper_ref[top : top + modes, left : left + modes] = -imag_part
            oper_ref[top : top + modes, right : right + modes] = real_part
            oper_ref[bottom : bottom + modes, left : left + modes] = -real_part
            oper_ref[bottom : bottom + modes, right : right + modes] = -imag_part
    product = times_operator(rows_ref[...], oper_ref[...])
    first_ref[...] = product.astype(BF16)
    wide_ref[...] = product


def times_operator(rows, operator):
    half = rows.shape[1] // 4
    upper = jnp.concatenate([rows[:, half : 2 * half], rows[:, 3 * half :]], axis=1)
    lower = jnp.concatenate([rows[:, :half], rows[:, 2 * half : 3 * half]], axis=1)
    both = jnp.dot(
        jnp.concatenate([upper, lower], axis=0), operator, preferred_element_type=F32
    )
    scale = 1.0 / math.sqrt(2.0 * half)
    count = rows.shape[0]
    above = both[:count] * scale
    below = both[count:] * (-scale)
    return jnp.concatenate([above[:, :half], below[:, :half], above[:, half:], below[:, half:]], 1)


def times_rows(left, right):
    order = left.shape[1] // 2
    count = left.shape[0]
    both = jnp.dot(
        jnp.concatenate([left[:, :order], left[:, order:]], axis=0),
        right,
        preferred_element_type=F32,
    )
    real_part = both[:count, :order] - both[count:, order:]
    imag_part = both[:count, order:] + both[count:, :order]
    return real_part, imag_part


def diagonal_sum(part, first_row):
    row = lax.broadcasted_iota(jnp.int32, part.shape, 0) + first_row
    column = lax.broadcasted_iota(jnp.int32, part.shape, 1)
    kept = jnp.where(row == column, part, 0.0)
    return jnp.sum(jnp.sum(kept, axis=0, keepdims=True), axis=1, keepdims=True)


def at_lanes(shape, values):
    lane = lax.broadcasted_iota(jnp.int32, shape, 1)
    total = jnp.zeros(shape, F32)
    for at, value in values:
        total = total + jnp.where(lane == at, value, 0.0)
    return total


def own_block(spaces, spins, space_step, spin_step):
    place = lax.rem(lax.axis_index("space") + space_step, spaces)
    spin = lax.rem(lax.axis_index("spin") + spin_step, spins)
    return place * spins + spin


def first_kernel(oper_ref, *refs):
    out_refs = list(refs[len(refs) // (PIECES + 1) :])
    for rows_ref in refs[: len(refs) // (PIECES + 1)]:
        product = times_operator(rows_ref[...], oper_ref[...]).astype(BF16)
        part = product.shape[0] // PIECES
        for piece in range(PIECES):
            out_refs.pop(0)[...] = product[piece * part : (piece + 1) * part]


def second_kernel(spaces, spins, next_ref, *refs):
    block_refs, (first_ref, second_ref, wide_ref) = list(refs[:-3]), refs[-3:]
    count = next_ref.shape[0]
    order = next_ref.shape[1] // 2
    for at in range(spaces * spins):
        start = own_block(spaces, spins, at // spins, at % spins) * count
        filled = 0
        while filled < count:
            block_ref = block_refs.pop(0)
            height = block_ref.shape[0]
            rows = pl.ds(pl.multiple_of(start + filled, height), height)
            first_ref[rows, :] = block_ref[...]
            filled += height
    real_part, imag_part = times_rows(next_ref[...], first_ref[...])
    second_ref[:, :order] = real_part.astype(BF16)
    second_ref[:, order:] = imag_part.astype(BF16)
    wide_ref[:, :order] = real_part
    wide_ref[:, order:] = imag_part


def turn_kernel(spaces, spins, offsets_ref, times_ref, first_ref, elem_ref, *refs):
    one_ref, two_ref, out_ref, weights_ref, share_ref, trace_ref, wide_ref = refs
    count, width = out_ref.shape
    order, lanes = width // 2, wide_ref.shape[0]
    first_row = own_block(spaces, spins, 0, 0) * count
    start = pl.multiple_of(first_row // lanes * lanes, lanes)
    for part in range(2):
        block = first_ref[:, pl.ds(pl.multiple_of(start + part * order, lanes), lanes)]
        wide_ref[:, part * order : (part + 1) * order] = block.astype(F32).T
    rows = pl.ds(pl.multiple_of(first_row - start, count), count)
    out_ref[...] = wide_ref[rows, :].astype(BF16)
    values = []
    for at, part_ref in enumerate((one_ref, two_ref)):
        values.append((2 * at, diagonal_sum(part_ref[:, :order], first_row)))
        values.append((2 * at + 1, diagonal_sum(part_ref[:, order:], first_row)))
    trace_ref[...] = at_lanes(trace_ref.shape, values)
    lane = lax.broadcasted_iota(jnp.int32, weights_ref.shape, 1)
    row = lax.broadcasted_iota(jnp.int32, weights_ref.shape, 0)
    counts = jnp.zeros(weights_ref.shape, F32)
    for j in range(offsets_ref.shape[0]):
        counts = counts + jnp.where(lane // 2 == offsets_ref[j], 1.0, 0.0)
    counts = jnp.where((lane < 6) & (lane % 2 == row), counts, 0.0)
    weights_ref[...] = counts
    here = jnp.where(times_ref[...] == lax.axis_index("tm"), 1.0, 0.0)
    weights_ref[2:3, : here.shape[1]] = here
    rows, columns = share_ref.shape[0], share_ref.shape[3]
    modes = elem_ref.shape[3]
    top = pl.multiple_of(lax.axis_index("space") * rows, rows)
    turn = lax.rem(modes - lax.axis_index("spin") * columns, modes)
    for direction in range(3):
        for part in range(2):
            block = elem_ref[direction, part, pl.ds(top, rows), :]
            share_ref[:, direction, part, :] = pltpu.roll(block, turn, 1)[:, :columns]


def whole_sum(values):
    return jnp.sum(jnp.sum(values, axis=0, keepdims=True), axis=1, keepdims=True)


def share_kernel(weights_ref, second_ref, turned_ref, early_ref, out_ref):
    order = second_ref.shape[1] // 2
    left_real, left_imag = second_ref[:, :order].astype(F32), second_ref[:, order:].astype(F32)
    right_real, right_imag = turned_ref[:, :order].astype(F32), turned_ref[:, order:].astype(F32)
    real_part = whole_sum(left_real * right_real - left_imag * right_imag)
    imag_part = whole_sum(left_real * right_imag + left_imag * right_real)
    traces = early_ref[0:1, :] + at_lanes((1, 128), [(4, real_part), (5, imag_part)])
    values = jnp.sum(traces * weights_ref[0:2, :], axis=1, keepdims=True)
    out_ref[...] = values * weights_ref[2:3, : out_ref.shape[1]]


def third_kernel(second_ref, first_ref, chain_ref):
    order = second_ref.shape[1] // 2
    real_part, imag_part = times_rows(second_ref[...], first_ref[...])
    scale = math.sqrt(order)
    chain_ref[:, :order] = (real_part * scale).astype(BF16)
    chain_ref[:, order:] = (imag_part * scale).astype(BF16)


def on_device(
    eigenvectors, gauge_links, perambulators, source_times, insert_offsets, derivative_dirs
):
    spaces, spins, slots = lax.axis_size("space"), lax.axis_size("spin"), lax.axis_size("tm")
    planes, side, modes = eigenvectors.shape[3], eigenvectors.shape[4], eigenvectors.shape[6]
    cells = planes * side * side
    own_rows = perambulators[0]
    count, width = own_rows.shape
    order = width // 2

    field = eigenvectors.reshape((6 * cells, modes))
    fields = [field] + [from_offset(field, "space", step) for step in range(1, spaces)]
    link = jnp.swapaxes(gauge_links.reshape((54, planes, side * side)), 1, 2)
    link = vmem_call(
        links_kernel,
        jax.ShapeDtypeStruct((cells, modes), BF16),
        [pltpu.VMEM(link.shape, F32), pltpu.VMEM((cells, modes), F32)],
        10**9,
    )(link)
    links = [link] + [from_offset(link, "space", step) for step in range(1, spaces)]
    fields[0], own_slab = vmem_call(
        functools.partial(slab_kernel, side),
        (
            jax.ShapeDtypeStruct(field.shape, BF16),
            jax.ShapeDtypeStruct((18 * cells, modes), BF16),
        ),
        [],
        10**6,
    )(field, link)

    held_rows, own_slab = lax.optimization_barrier((own_rows, own_slab))
    far_rows = [from_offset(held_rows, "space", step) for step in range(1, spaces)]

    norm_scale = 1.0 / math.sqrt(6.0 * 4.0 * planes * spaces * side * side)
    rows_shape = jax.ShapeDtypeStruct((count, width), BF16)
    trace_shape = jax.ShapeDtypeStruct((8, 128), F32)
    elements = vmem_call(
        functools.partial(elementals_kernel, side, norm_scale, spaces),
        jax.ShapeDtypeStruct((3, 2, modes, modes), F32),
        [pltpu.VMEM((6 * cells * spaces, 6 * modes), BF16)],
        10**10,
    )(own_slab, *fields, *links)
    wide_shape = jax.ShapeDtypeStruct((count, width), F32)
    operator, own_first, own_wide = vmem_call(
        operator_kernel,
        (jax.ShapeDtypeStruct((4 * modes, 4 * modes), BF16), rows_shape, wide_shape),
        [],
        10**8,
        smem=(0,),
    )(derivative_dirs, elements, own_rows)

    next_first = from_offset(own_first, "tm", 1)

    far_rows, held_first = lax.optimization_barrier((far_rows, own_first))
    piece_shape = jax.ShapeDtypeStruct((count // PIECES, width), BF16)
    far_first = vmem_call(first_kernel, (piece_shape,) * (PIECES * len(far_rows)), [], 10**6)(
        operator, *far_rows
    )
    blocks = [own_first] + [from_offset(held_first, "spin", step) for step in range(1, spins)]
    for at in range(0, len(far_first), PIECES):
        pieces = list(far_first[at : at + PIECES])
        blocks += pieces
        for step in range(1, spins):
            blocks += [from_offset(piece, "spin", step) for piece in pieces]
    first, second, second_wide = vmem_call(
        functools.partial(second_kernel, spaces, spins),
        (jax.ShapeDtypeStruct((order, width), BF16), rows_shape, wide_shape),
        [],
        3 * 10**8,
    )(next_first, *blocks)
    next_second = from_offset(second, "tm", 1)

    turned, weights, elementals, early = vmem_call(
        functools.partial(turn_kernel, spaces, spins),
        (
            rows_shape,
            trace_shape,
            jax.ShapeDtypeStruct((modes // spaces, 3, 2, modes // spins), F32),
            trace_shape,
        ),
        [pltpu.VMEM((max(count, 128), width), F32)],
        10**6,
        smem=(0,),
    )(insert_offsets, source_times[None, :], first, elements, own_wide, second_wide)
    shares = vmem_call(
        share_kernel,
        jax.ShapeDtypeStruct((2, source_times.shape[0]), F32),
        [],
        10**6,
    )(weights, next_second, turned, early)
    chain = vmem_call(third_kernel, rows_shape, [], 10**8)(next_second, first)

    devices = slots * spaces * spins
    if devices & (devices - 1):
        shares = lax.psum(shares, ("tm", "space", "spin"))
    else:
        bits = [1 << at for at in range(devices.bit_length() - 1)]
        while bits:
            low, high = bits[0], bits[-1]
            bits = bits[1:-1]
            masks = [low] if low == high else [low, high, low | high]
            parts = [swapped(shares, devices, mask) for mask in masks]
            shares = functools.reduce(lambda x, y: x + y, parts, shares)
    return (elementals[None], chain[None], shares.T)


def solution(mesh):
    in_specs = (
        P(("cfg", "tm"), None, None, "space", None, None, None),
        P(("cfg", "tm"), None, None, None, None, "space", None),
        P(("cfg", "tm"), ("space", "spin"), None),
        P(),
        P(),
        P(),
    )
    out_specs = (
        P(("cfg", "tm"), "space", None, None, "spin"),
        P(("cfg", "tm"), ("space", "spin"), None),
        P("cfg", None),
    )
    return jax.shard_map(
        on_device, mesh=mesh, in_specs=in_specs, out_specs=out_specs, check_vma=False
    )
```

```python
import functools
import math

import jax
import jax.numpy as jnp
from jax import lax
from jax.experimental import pallas as pl
from jax.experimental.pallas import tpu as pltpu

from jax.sharding import PartitionSpec as P

F32 = jnp.float32
BF16 = jnp.bfloat16
PIECES = 2


def from_offset(block, axis, distance):
    count = lax.axis_size(axis)
    return lax.ppermute(block, axis, [((i + distance) % count, i) for i in range(count)])


def swapped(block, devices, mask):
    return lax.ppermute(block, ("tm", "space", "spin"), [(i ^ mask, i) for i in range(devices)])


def vmem_call(kernel, out_shape, scratch, flops, smem=()):
    def call(*operands):
        specs = [
            pl.BlockSpec(memory_space=pltpu.SMEM if i in smem else pltpu.VMEM)
            for i in range(len(operands))
        ]
        outs = jax.tree.map(lambda _: pl.BlockSpec(memory_space=pltpu.VMEM), out_shape)
        return pl.pallas_call(
            kernel,
            out_shape=out_shape,
            in_specs=specs,
            out_specs=outs,
            scratch_shapes=scratch,
            compiler_params=pltpu.CompilerParams(vmem_limit_bytes=16 * 1024 * 1024),
            cost_estimate=pl.CostEstimate(
                flops=flops, bytes_accessed=1 << 20, transcendentals=0
            ),
        )(*operands)

    return call


def moved(field, distance):
    rows = field.shape[0]
    return pltpu.roll(field, distance % rows, 0) if distance % rows else field


def ahead_of(field, stride, side):
    row = lax.broadcasted_iota(jnp.int32, field.shape, 0)
    last = (row // stride) % side == side - 1
    return jnp.where(last, moved(field, (side - 1) * stride), moved(field, -stride))


def behind_of(field, stride, side):
    row = lax.broadcasted_iota(jnp.int32, field.shape, 0)
    start = (row // stride) % side == 0
    return jnp.where(start, moved(field, (1 - side) * stride), moved(field, stride))


def links_kernel(links_ref, out_ref, wide_ref, turned_ref):
    coefficients, cross, planes = links_ref.shape
    wide_ref[...] = links_ref[...].astype(F32)
    for at in range(cross):
        rows = pl.ds(at, planes, stride=cross)
        turned_ref[rows, :coefficients] = wide_ref[:, at, :].T
    out_ref[...] = turned_ref[...].astype(BF16)


def link_at(links, direction, colour, other):
    at = direction * 18 + colour * 3 + other
    return links[:, at : at + 1], links[:, at + 9 : at + 10]


def added(total, term):
    return term if total is None else total + term


def times_links(links, direction, vectors):
    parts = [None] * 6
    for colour in range(3):
        for other in range(3):
            real, imag = link_at(links, direction, colour, other)
            real_part, imag_part = vectors[other], vectors[3 + other]
            parts[colour] = added(parts[colour], real * real_part - imag * imag_part)
            parts[3 + colour] = added(parts[3 + colour], real * imag_part + imag * real_part)
    return parts


def times_adjoint(links, direction, vectors):
    parts = [None] * 6
    for colour in range(3):
        for other in range(3):
            real, imag = link_at(links, direction, colour, other)
            real_part, imag_part = vectors[colour], vectors[3 + colour]
            parts[other] = added(parts[other], real * real_part + imag * imag_part)
            parts[3 + other] = added(parts[3 + other], real * imag_part - imag * real_part)
    return [part.astype(BF16) for part in parts]


def across_slab(links, direction, vectors, side):
    stride = side**direction
    forward = times_links(links, direction, [ahead_of(v, stride, side) for v in vectors])
    adjoint = times_adjoint(links, direction, vectors)
    return [
        (part - behind_of(back.astype(F32), stride, side)).astype(BF16)
        for part, back in zip(forward, adjoint)
    ]


def slab_fields(ref):
    cells = ref.shape[0] // 6
    return [ref[k * cells : (k + 1) * cells, :].astype(F32) for k in range(6)]


def slab_kernel(side, vectors_ref, links_ref, copy_ref, out_ref):
    vectors = slab_fields(vectors_ref)
    links = links_ref[...].astype(F32)
    cells = links.shape[0]
    copy_ref[...] = vectors_ref[...]
    parts = across_slab(links, 0, vectors, side) + across_slab(links, 1, vectors, side)
    parts += times_adjoint(links, 2, vectors)
    for at, part in enumerate(parts):
        out_ref[at * cells : (at + 1) * cells, :] = part


def elementals_kernel(side, scale, slabs, early_ref, *refs):
    vector_refs, link_refs, out_refs = refs[:slabs], refs[slabs : 2 * slabs], refs[2 * slabs :]
    elem_ref, rhs_ref = out_refs
    modes = elem_ref.shape[-1]
    cells = link_refs[0].shape[0]
    sites = slabs * cells

    def put(slab, direction, parts):
        left, right = 2 * direction * modes, (2 * direction + 1) * modes
        for colour in range(3):
            low = colour * sites + slab * cells
            high = low + 3 * sites
            real_part, imag_part = parts[colour], parts[3 + colour]
            rhs_ref[low : low + cells, left : left + modes] = real_part
            rhs_ref[high : high + cells, left : left + modes] = imag_part
            rhs_ref[low : low + cells, right : right + modes] = imag_part
            rhs_ref[high : high + cells, right : right + modes] = -real_part

    early = [early_ref[at * cells : (at + 1) * cells, :] for at in range(18)]
    put(0, 0, early[:6])
    put(0, 1, early[6:12])
    vectors = [slab_fields(ref) for ref in vector_refs]
    links = [ref[...].astype(F32) for ref in link_refs]
    adjoint = [early[12:]]
    for slab in range(1, slabs):
        put(slab, 0, across_slab(links[slab], 0, vectors[slab], side))
        put(slab, 1, across_slab(links[slab], 1, vectors[slab], side))
        adjoint.append(times_adjoint(links[slab], 2, vectors[slab]))
    plane = side * side
    for slab in range(slabs):
        after, before = (slab + 1) % slabs, (slab - 1) % slabs
        ahead = [
            jnp.concatenate([here[plane:], there[:plane]], axis=0)
            for here, there in zip(vectors[slab], vectors[after])
        ]
        forward = times_links(links[slab], 2, ahead)
        parts = []
        for k in range(6):
            here, there = adjoint[slab][k].astype(F32), adjoint[before][k].astype(F32)
            behind = jnp.concatenate([there[cells - plane :], here[: cells - plane]], axis=0)
            parts.append((forward[k] - behind).astype(BF16))
        put(slab, 2, parts)

    fields = [ref[k * cells : (k + 1) * cells, :] for k in range(6) for ref in vector_refs]
    vectors = jnp.concatenate(fields, axis=0)
    product = lax.dot_general(
        vectors, rhs_ref[...], (((0,), (0,)), ((), ())), preferred_element_type=F32
    )
    for direction in range(3):
        left = 2 * direction * modes
        real_part = product[:, left : left + modes] * scale
        imag_part = product[:, left + modes : left + 2 * modes] * scale
        elem_ref[direction, 0] = real_part
        elem_ref[direction, 1] = imag_part


def operator_kernel(
    dirs_ref, elem_ref, rows_ref, oper_ref, first_ref, wide_ref, copy_ref
):
    modes = elem_ref.shape[-1]
    copy_ref[...] = rows_ref[...]
    picked = []
    for k in range(3):
        for part in range(2):
            picked.append(elem_ref[dirs_ref[k], part].astype(BF16).astype(F32))
    zero_real, zero_imag, one_real, one_imag, two_real, two_imag = picked
    sum_real = [[two_real, zero_real + one_imag], [zero_real - one_imag, -two_real]]
    sum_imag = [[two_imag, zero_imag - one_real], [zero_imag + one_real, -two_imag]]
    for p in range(2):
        for q in range(2):
            top, bottom = p * modes, (2 + p) * modes
            left, right = q * modes, (2 + q) * modes
            real_part = sum_real[p][q].astype(BF16)
            imag_part = sum_imag[p][q].astype(BF16)
            oper_ref[top : top + modes, left : left + modes] = -imag_part
            oper_ref[top : top + modes, right : right + modes] = real_part
            oper_ref[bottom : bottom + modes, left : left + modes] = -real_part
            oper_ref[bottom : bottom + modes, right : right + modes] = -imag_part
    product = times_operator(rows_ref[...], oper_ref[...])
    first_ref[...] = product.astype(BF16)
    wide_ref[...] = product


def times_operator(rows, operator):
    half = rows.shape[1] // 4
    upper = jnp.concatenate([rows[:, half : 2 * half], rows[:, 3 * half :]], axis=1)
    lower = jnp.concatenate([rows[:, :half], rows[:, 2 * half : 3 * half]], axis=1)
    both = jnp.dot(
        jnp.concatenate([upper, lower], axis=0), operator, preferred_element_type=F32
    )
    scale = 1.0 / math.sqrt(2.0 * half)
    count = rows.shape[0]
    above = both[:count] * scale
    below = both[count:] * (-scale)
    return jnp.concatenate([above[:, :half], below[:, :half], above[:, half:], below[:, half:]], 1)


def times_rows(left, right):
    order = left.shape[1] // 2
    count = left.shape[0]
    both = jnp.dot(
        jnp.concatenate([left[:, :order], left[:, order:]], axis=0),
        right,
        preferred_element_type=F32,
    )
    real_part = both[:count, :order] - both[count:, order:]
    imag_part = both[:count, order:] + both[count:, :order]
    return real_part, imag_part


def diagonal_sum(part, first_row):
    row = lax.broadcasted_iota(jnp.int32, part.shape, 0) + first_row
    column = lax.broadcasted_iota(jnp.int32, part.shape, 1)
    kept = jnp.where(row == column, part, 0.0)
    return jnp.sum(jnp.sum(kept, axis=0, keepdims=True), axis=1, keepdims=True)


def at_lanes(shape, values):
    lane = lax.broadcasted_iota(jnp.int32, shape, 1)
    total = jnp.zeros(shape, F32)
    for at, value in values:
        total = total + jnp.where(lane == at, value, 0.0)
    return total


def own_block(spaces, spins, space_step, spin_step):
    place = lax.rem(lax.axis_index("space") + space_step, spaces)
    spin = lax.rem(lax.axis_index("spin") + spin_step, spins)
    return place * spins + spin


def first_kernel(spaces, spins, oper_ref, own_ref, *refs):
    block_refs, first_ref = refs[:-1], refs[-1]
    count = own_ref.shape[0]
    start = pl.multiple_of(own_block(spaces, spins, 0, 0) * count, count)
    first_ref[pl.ds(start, count), :] = own_ref[...]
    at = 1
    left = list(block_refs)
    while left:
        rows = left.pop(0)[...]
        while rows.shape[0] < count:
            rows = jnp.concatenate([rows, left.pop(0)[...]], axis=0)
        product = times_operator(rows, oper_ref[...])
        start = pl.multiple_of(own_block(spaces, spins, at // spins, at % spins) * count, count)
        first_ref[pl.ds(start, count), :] = product.astype(BF16)
        at += 1


def second_kernel(next_ref, first_ref, second_ref, wide_ref):
    order = next_ref.shape[1] // 2
    real_part, imag_part = times_rows(next_ref[...], first_ref[...])
    second_ref[:, :order] = real_part.astype(BF16)
    second_ref[:, order:] = imag_part.astype(BF16)
    wide_ref[:, :order] = real_part
    wide_ref[:, order:] = imag_part


def turn_kernel(spaces, spins, offsets_ref, times_ref, first_ref, elem_ref, *refs):
    one_ref, two_ref, out_ref, weights_ref, share_ref, trace_ref, wide_ref = refs
    count, width = out_ref.shape
    order, lanes = width // 2, wide_ref.shape[0]
    first_row = own_block(spaces, spins, 0, 0) * count
    start = pl.multiple_of(first_row // lanes * lanes, lanes)
    for part in range(2):
        block = first_ref[:, pl.ds(pl.multiple_of(start + part * order, lanes), lanes)]
        wide_ref[:, part * order : (part + 1) * order] = block.astype(F32).T
    rows = pl.ds(pl.multiple_of(first_row - start, count), count)
    out_ref[...] = wide_ref[rows, :].astype(BF16)
    values = []
    for at, part_ref in enumerate((one_ref, two_ref)):
        values.append((2 * at, diagonal_sum(part_ref[:, :order], first_row)))
        values.append((2 * at + 1, diagonal_sum(part_ref[:, order:], first_row)))
    trace_ref[...] = at_lanes(trace_ref.shape, values)
    lane = lax.broadcasted_iota(jnp.int32, weights_ref.shape, 1)
    row = lax.broadcasted_iota(jnp.int32, weights_ref.shape, 0)
    counts = jnp.zeros(weights_ref.shape, F32)
    for j in range(offsets_ref.shape[0]):
        counts = counts + jnp.where(lane // 2 == offsets_ref[j], 1.0, 0.0)
    counts = jnp.where((lane < 6) & (lane % 2 == row), counts, 0.0)
    weights_ref[...] = counts
    here = jnp.where(times_ref[...] == lax.axis_index("tm"), 1.0, 0.0)
    weights_ref[2:3, : here.shape[1]] = here
    rows, columns = share_ref.shape[0], share_ref.shape[3]
    modes = elem_ref.shape[3]
    top = pl.multiple_of(lax.axis_index("space") * rows, rows)
    turn = lax.rem(modes - lax.axis_index("spin") * columns, modes)
    for direction in range(3):
        for part in range(2):
            block = elem_ref[direction, part, pl.ds(top, rows), :]
            share_ref[:, direction, part, :] = pltpu.roll(block, turn, 1)[:, :columns]


def whole_sum(values):
    return jnp.sum(jnp.sum(values, axis=0, keepdims=True), axis=1, keepdims=True)


def share_kernel(weights_ref, second_ref, turned_ref, early_ref, out_ref):
    order = second_ref.shape[1] // 2
    left_real, left_imag = second_ref[:, :order].astype(F32), second_ref[:, order:].astype(F32)
    right_real, right_imag = turned_ref[:, :order].astype(F32), turned_ref[:, order:].astype(F32)
    real_part = whole_sum(left_real * right_real - left_imag * right_imag)
    imag_part = whole_sum(left_real * right_imag + left_imag * right_real)
    traces = early_ref[0:1, :] + at_lanes((1, 128), [(4, real_part), (5, imag_part)])
    values = jnp.sum(traces * weights_ref[0:2, :], axis=1, keepdims=True)
    out_ref[...] = values * weights_ref[2:3, : out_ref.shape[1]]


def third_kernel(second_ref, first_ref, chain_ref):
    order = second_ref.shape[1] // 2
    real_part, imag_part = times_rows(second_ref[...], first_ref[...])
    scale = math.sqrt(order)
    chain_ref[:, :order] = (real_part * scale).astype(BF16)
    chain_ref[:, order:] = (imag_part * scale).astype(BF16)


def on_device(
    eigenvectors, gauge_links, perambulators, source_times, insert_offsets, derivative_dirs
):
    spaces, spins, slots = lax.axis_size("space"), lax.axis_size("spin"), lax.axis_size("tm")
    planes, side, modes = eigenvectors.shape[3], eigenvectors.shape[4], eigenvectors.shape[6]
    cells = planes * side * side
    own_rows = perambulators[0]
    count, width = own_rows.shape
    order = width // 2

    field = eigenvectors.reshape((6 * cells, modes))
    fields = [field] + [from_offset(field, "space", step) for step in range(1, spaces)]
    link = jnp.swapaxes(gauge_links.reshape((54, planes, side * side)), 1, 2)
    link = vmem_call(
        links_kernel,
        jax.ShapeDtypeStruct((cells, modes), BF16),
        [pltpu.VMEM(link.shape, F32), pltpu.VMEM((cells, modes), F32)],
        10**9,
    )(link)
    links = [link] + [from_offset(link, "space", step) for step in range(1, spaces)]
    fields[0], own_slab = vmem_call(
        functools.partial(slab_kernel, side),
        (
            jax.ShapeDtypeStruct(field.shape, BF16),
            jax.ShapeDtypeStruct((18 * cells, modes), BF16),
        ),
        [],
        10**6,
    )(field, link)

    held_rows, own_slab = lax.optimization_barrier((own_rows, own_slab))
    far_rows = [from_offset(held_rows, "space", step) for step in range(1, spaces)]

    norm_scale = 1.0 / math.sqrt(6.0 * 4.0 * planes * spaces * side * side)
    rows_shape = jax.ShapeDtypeStruct((count, width), BF16)
    trace_shape = jax.ShapeDtypeStruct((8, 128), F32)
    elements = vmem_call(
        functools.partial(elementals_kernel, side, norm_scale, spaces),
        jax.ShapeDtypeStruct((3, 2, modes, modes), F32),
        [pltpu.VMEM((6 * cells * spaces, 6 * modes), BF16)],
        10**10,
    )(own_slab, *fields, *links)
    wide_shape = jax.ShapeDtypeStruct((count, width), F32)
    operator, own_first, own_wide, rows_copy = vmem_call(
        operator_kernel,
        (jax.ShapeDtypeStruct((4 * modes, 4 * modes), BF16), rows_shape, wide_shape, rows_shape),
        [],
        10**8,
        smem=(0,),
    )(derivative_dirs, elements, own_rows)

    next_first = from_offset(own_first, "tm", 1)

    far_rows, held_rows, held_first = lax.optimization_barrier((far_rows, rows_copy, own_first))
    blocks = []
    for at, block in enumerate([held_rows] + far_rows):
        blocks += [block]
        pieces = PIECES if at else 1
        for step in range(1, spins):
            for piece in range(pieces):
                low, high = piece * count // pieces, (piece + 1) * count // pieces
                blocks += [from_offset(block[low:high], "spin", step)]
    blocks = blocks[1:]
    first = vmem_call(
        functools.partial(first_kernel, spaces, spins),
        jax.ShapeDtypeStruct((order, width), BF16),
        [],
        10**6,
    )(operator, held_first, *blocks)

    second, second_wide = vmem_call(
        second_kernel,
        (rows_shape, wide_shape),
        [],
        3 * 10**8,
    )(next_first, first)

    next_second = from_offset(second, "tm", 1)

    turned, weights, elementals, early = vmem_call(
        functools.partial(turn_kernel, spaces, spins),
        (
            rows_shape,
            trace_shape,
            jax.ShapeDtypeStruct((modes // spaces, 3, 2, modes // spins), F32),
            trace_shape,
        ),
        [pltpu.VMEM((max(count, 128), width), F32)],
        10**6,
        smem=(0,),
    )(insert_offsets, source_times[None, :], first, elements, own_wide, second_wide)
    shares = vmem_call(
        share_kernel,
        jax.ShapeDtypeStruct((2, source_times.shape[0]), F32),
        [],
        10**6,
    )(weights, next_second, turned, early)

    devices = slots * spaces * spins
    if devices & (devices - 1):
        shares = lax.psum(shares, ("tm", "space", "spin"))
    else:
        bits = [1 << at for at in range(devices.bit_length() - 1)]
        while bits:
            low, high = bits[0], bits[-1]
            bits = bits[1:-1]
            masks = [low] if low == high else [low, high, low | high]
            parts = [swapped(shares, devices, mask) for mask in masks]
            shares = functools.reduce(lambda x, y: x + y, parts, shares)
            if high == devices >> 1:
                shares, next_second = lax.optimization_barrier((shares, next_second))
    chain = vmem_call(third_kernel, rows_shape, [], 10**8)(next_second, first)
    return (elementals[None], chain[None], shares.T)


def solution(mesh):
    in_specs = (
        P(("cfg", "tm"), None, None, "space", None, None, None),
        P(("cfg", "tm"), None, None, None, None, "space", None),
        P(("cfg", "tm"), ("space", "spin"), None),
        P(),
        P(),
        P(),
    )
    out_specs = (
        P(("cfg", "tm"), "space", None, None, "spin"),
        P(("cfg", "tm"), ("space", "spin"), None),
        P("cfg", None),
    )
    return jax.shard_map(
        on_device, mesh=mesh, in_specs=in_specs, out_specs=out_specs, check_vma=False
    )
```

```python
import functools
import math

import jax
import jax.numpy as jnp
from jax import lax
from jax.experimental import pallas as pl
from jax.experimental.pallas import tpu as pltpu

from jax.sharding import PartitionSpec as P

F32 = jnp.float32
BF16 = jnp.bfloat16
PIECES = 1


def from_offset(block, axis, distance):
    count = lax.axis_size(axis)
    return lax.ppermute(block, axis, [((i + distance) % count, i) for i in range(count)])


def swapped(block, devices, mask):
    return lax.ppermute(block, ("tm", "space", "spin"), [(i ^ mask, i) for i in range(devices)])


def vmem_call(kernel, out_shape, scratch, flops, smem=()):
    def call(*operands):
        specs = [
            pl.BlockSpec(memory_space=pltpu.SMEM if i in smem else pltpu.VMEM)
            for i in range(len(operands))
        ]
        outs = jax.tree.map(lambda _: pl.BlockSpec(memory_space=pltpu.VMEM), out_shape)
        return pl.pallas_call(
            kernel,
            out_shape=out_shape,
            in_specs=specs,
            out_specs=outs,
            scratch_shapes=scratch,
            compiler_params=pltpu.CompilerParams(vmem_limit_bytes=16 * 1024 * 1024),
            cost_estimate=pl.CostEstimate(
                flops=flops, bytes_accessed=1 << 20, transcendentals=0
            ),
        )(*operands)

    return call


def moved(field, distance):
    rows = field.shape[0]
    return pltpu.roll(field, distance % rows, 0) if distance % rows else field


def ahead_of(field, stride, side):
    row = lax.broadcasted_iota(jnp.int32, field.shape, 0)
    last = (row // stride) % side == side - 1
    return jnp.where(last, moved(field, (side - 1) * stride), moved(field, -stride))


def behind_of(field, stride, side):
    row = lax.broadcasted_iota(jnp.int32, field.shape, 0)
    start = (row // stride) % side == 0
    return jnp.where(start, moved(field, (1 - side) * stride), moved(field, stride))


def links_kernel(links_ref, out_ref, wide_ref, turned_ref):
    coefficients, cross, planes = links_ref.shape
    wide_ref[...] = links_ref[...].astype(F32)
    for at in range(cross):
        rows = pl.ds(at, planes, stride=cross)
        turned_ref[rows, :coefficients] = wide_ref[:, at, :].T
    out_ref[...] = turned_ref[...].astype(BF16)


def link_at(links, direction, colour, other):
    at = direction * 18 + colour * 3 + other
    return links[:, at : at + 1], links[:, at + 9 : at + 10]


def added(total, term):
    return term if total is None else total + term


def times_links(links, direction, vectors):
    parts = [None] * 6
    for colour in range(3):
        for other in range(3):
            real, imag = link_at(links, direction, colour, other)
            real_part, imag_part = vectors[other], vectors[3 + other]
            parts[colour] = added(parts[colour], real * real_part - imag * imag_part)
            parts[3 + colour] = added(parts[3 + colour], real * imag_part + imag * real_part)
    return parts


def times_adjoint(links, direction, vectors):
    parts = [None] * 6
    for colour in range(3):
        for other in range(3):
            real, imag = link_at(links, direction, colour, other)
            real_part, imag_part = vectors[colour], vectors[3 + colour]
            parts[other] = added(parts[other], real * real_part + imag * imag_part)
            parts[3 + other] = added(parts[3 + other], real * imag_part - imag * real_part)
    return [part.astype(BF16) for part in parts]


def across_slab(links, direction, vectors, side):
    stride = side**direction
    forward = times_links(links, direction, [ahead_of(v, stride, side) for v in vectors])
    adjoint = times_adjoint(links, direction, vectors)
    return [
        (part - behind_of(back.astype(F32), stride, side)).astype(BF16)
        for part, back in zip(forward, adjoint)
    ]


def slab_fields(ref):
    cells = ref.shape[0] // 6
    return [ref[k * cells : (k + 1) * cells, :].astype(F32) for k in range(6)]


def slab_kernel(side, vectors_ref, links_ref, copy_ref, out_ref):
    vectors = slab_fields(vectors_ref)
    links = links_ref[...].astype(F32)
    cells = links.shape[0]
    copy_ref[...] = vectors_ref[...]
    parts = across_slab(links, 0, vectors, side) + across_slab(links, 1, vectors, side)
    parts += times_adjoint(links, 2, vectors)
    for at, part in enumerate(parts):
        out_ref[at * cells : (at + 1) * cells, :] = part


def elementals_kernel(side, scale, slabs, early_ref, *refs):
    vector_refs, link_refs, out_refs = refs[:slabs], refs[slabs : 2 * slabs], refs[2 * slabs :]
    elem_ref, rhs_ref = out_refs
    modes = elem_ref.shape[-1]
    cells = link_refs[0].shape[0]
    sites = slabs * cells

    def put(slab, direction, parts):
        left, right = 2 * direction * modes, (2 * direction + 1) * modes
        for colour in range(3):
            low = colour * sites + slab * cells
            high = low + 3 * sites
            real_part, imag_part = parts[colour], parts[3 + colour]
            rhs_ref[low : low + cells, left : left + modes] = real_part
            rhs_ref[high : high + cells, left : left + modes] = imag_part
            rhs_ref[low : low + cells, right : right + modes] = imag_part
            rhs_ref[high : high + cells, right : right + modes] = -real_part

    early = [early_ref[at * cells : (at + 1) * cells, :] for at in range(18)]
    put(0, 0, early[:6])
    put(0, 1, early[6:12])
    vectors = [slab_fields(ref) for ref in vector_refs]
    links = [ref[...].astype(F32) for ref in link_refs]
    adjoint = [early[12:]]
    for slab in range(1, slabs):
        put(slab, 0, across_slab(links[slab], 0, vectors[slab], side))
        put(slab, 1, across_slab(links[slab], 1, vectors[slab], side))
        adjoint.append(times_adjoint(links[slab], 2, vectors[slab]))
    plane = side * side
    for slab in range(slabs):
        after, before = (slab + 1) % slabs, (slab - 1) % slabs
        ahead = [
            jnp.concatenate([here[plane:], there[:plane]], axis=0)
            for here, there in zip(vectors[slab], vectors[after])
        ]
        forward = times_links(links[slab], 2, ahead)
        parts = []
        for k in range(6):
            here, there = adjoint[slab][k].astype(F32), adjoint[before][k].astype(F32)
            behind = jnp.concatenate([there[cells - plane :], here[: cells - plane]], axis=0)
            parts.append((forward[k] - behind).astype(BF16))
        put(slab, 2, parts)

    fields = [ref[k * cells : (k + 1) * cells, :] for k in range(6) for ref in vector_refs]
    vectors = jnp.concatenate(fields, axis=0)
    product = lax.dot_general(
        vectors, rhs_ref[...], (((0,), (0,)), ((), ())), preferred_element_type=F32
    )
    for direction in range(3):
        left = 2 * direction * modes
        real_part = product[:, left : left + modes] * scale
        imag_part = product[:, left + modes : left + 2 * modes] * scale
        elem_ref[direction, 0] = real_part
        elem_ref[direction, 1] = imag_part


def operator_kernel(
    dirs_ref, elem_ref, rows_ref, oper_ref, first_ref, wide_ref
):
    modes = elem_ref.shape[-1]
    picked = []
    for k in range(3):
        for part in range(2):
            picked.append(elem_ref[dirs_ref[k], part].astype(BF16).astype(F32))
    zero_real, zero_imag, one_real, one_imag, two_real, two_imag = picked
    sum_real = [[two_real, zero_real + one_imag], [zero_real - one_imag, -two_real]]
    sum_imag = [[two_imag, zero_imag - one_real], [zero_imag + one_real, -two_imag]]
    for p in range(2):
        for q in range(2):
            top, bottom = p * modes, (2 + p) * modes
            left, right = q * modes, (2 + q) * modes
            real_part = sum_real[p][q].astype(BF16)
            imag_part = sum_imag[p][q].astype(BF16)
            oper_ref[top : top + modes, left : left + modes] = -imag_part
            oper_ref[top : top + modes, right : right + modes] = real_part
            oper_ref[bottom : bottom + modes, left : left + modes] = -real_part
            oper_ref[bottom : bottom + modes, right : right + modes] = -imag_part
    product = times_operator(rows_ref[...], oper_ref[...])
    first_ref[...] = product.astype(BF16)
    wide_ref[...] = product


def times_operator(rows, operator):
    half = rows.shape[1] // 4
    upper = jnp.concatenate([rows[:, half : 2 * half], rows[:, 3 * half :]], axis=1)
    lower = jnp.concatenate([rows[:, :half], rows[:, 2 * half : 3 * half]], axis=1)
    both = jnp.dot(
        jnp.concatenate([upper, lower], axis=0), operator, preferred_element_type=F32
    )
    scale = 1.0 / math.sqrt(2.0 * half)
    count = rows.shape[0]
    above = both[:count] * scale
    below = both[count:] * (-scale)
    return jnp.concatenate([above[:, :half], below[:, :half], above[:, half:], below[:, half:]], 1)


def times_rows(left, right):
    order = left.shape[1] // 2
    count = left.shape[0]
    both = jnp.dot(
        jnp.concatenate([left[:, :order], left[:, order:]], axis=0),
        right,
        preferred_element_type=F32,
    )
    real_part = both[:count, :order] - both[count:, order:]
    imag_part = both[:count, order:] + both[count:, :order]
    return real_part, imag_part


def diagonal_sum(part, first_row):
    row = lax.broadcasted_iota(jnp.int32, part.shape, 0) + first_row
    column = lax.broadcasted_iota(jnp.int32, part.shape, 1)
    kept = jnp.where(row == column, part, 0.0)
    return jnp.sum(jnp.sum(kept, axis=0, keepdims=True), axis=1, keepdims=True)


def at_lanes(shape, values):
    lane = lax.broadcasted_iota(jnp.int32, shape, 1)
    total = jnp.zeros(shape, F32)
    for at, value in values:
        total = total + jnp.where(lane == at, value, 0.0)
    return total


def own_block(spaces, spins, space_step, spin_step):
    place = lax.rem(lax.axis_index("space") + space_step, spaces)
    spin = lax.rem(lax.axis_index("spin") + spin_step, spins)
    return place * spins + spin


def first_kernel(oper_ref, *refs):
    out_refs = list(refs[len(refs) // (PIECES + 1) :])
    for rows_ref in refs[: len(refs) // (PIECES + 1)]:
        product = times_operator(rows_ref[...], oper_ref[...]).astype(BF16)
        part = product.shape[0] // PIECES
        for piece in range(PIECES):
            out_refs.pop(0)[...] = product[piece * part : (piece + 1) * part]


def second_kernel(spaces, spins, next_ref, *refs):
    block_refs, (first_ref, second_ref, wide_ref) = list(refs[:-3]), refs[-3:]
    count = next_ref.shape[0]
    order = next_ref.shape[1] // 2
    for at in range(spaces * spins):
        start = own_block(spaces, spins, at // spins, at % spins) * count
        filled = 0
        while filled < count:
            block_ref = block_refs.pop(0)
            height = block_ref.shape[0]
            rows = pl.ds(pl.multiple_of(start + filled, height), height)
            first_ref[rows, :] = block_ref[...]
            filled += height
    real_part, imag_part = times_rows(next_ref[...], first_ref[...])
    second_ref[:, :order] = real_part.astype(BF16)
    second_ref[:, order:] = imag_part.astype(BF16)
    wide_ref[:, :order] = real_part
    wide_ref[:, order:] = imag_part


def turn_kernel(spaces, spins, offsets_ref, times_ref, first_ref, elem_ref, *refs):
    one_ref, two_ref, out_ref, weights_ref, share_ref, trace_ref, wide_ref = refs
    count, width = out_ref.shape
    order, lanes = width // 2, wide_ref.shape[0]
    first_row = own_block(spaces, spins, 0, 0) * count
    start = pl.multiple_of(first_row // lanes * lanes, lanes)
    for part in range(2):
        block = first_ref[:, pl.ds(pl.multiple_of(start + part * order, lanes), lanes)]
        wide_ref[:, part * order : (part + 1) * order] = block.astype(F32).T
    rows = pl.ds(pl.multiple_of(first_row - start, count), count)
    out_ref[...] = wide_ref[rows, :].astype(BF16)
    values = []
    for at, part_ref in enumerate((one_ref, two_ref)):
        values.append((2 * at, diagonal_sum(part_ref[:, :order], first_row)))
        values.append((2 * at + 1, diagonal_sum(part_ref[:, order:], first_row)))
    trace_ref[...] = at_lanes(trace_ref.shape, values)
    lane = lax.broadcasted_iota(jnp.int32, weights_ref.shape, 1)
    row = lax.broadcasted_iota(jnp.int32, weights_ref.shape, 0)
    counts = jnp.zeros(weights_ref.shape, F32)
    for j in range(offsets_ref.shape[0]):
        counts = counts + jnp.where(lane // 2 == offsets_ref[j], 1.0, 0.0)
    counts = jnp.where((lane < 6) & (lane % 2 == row), counts, 0.0)
    weights_ref[...] = counts
    here = jnp.where(times_ref[...] == lax.axis_index("tm"), 1.0, 0.0)
    weights_ref[2:3, : here.shape[1]] = here
    rows, columns = share_ref.shape[0], share_ref.shape[3]
    modes = elem_ref.shape[3]
    top = pl.multiple_of(lax.axis_index("space") * rows, rows)
    turn = lax.rem(modes - lax.axis_index("spin") * columns, modes)
    for direction in range(3):
        for part in range(2):
            block = elem_ref[direction, part, pl.ds(top, rows), :]
            share_ref[:, direction, part, :] = pltpu.roll(block, turn, 1)[:, :columns]


def whole_sum(values):
    return jnp.sum(jnp.sum(values, axis=0, keepdims=True), axis=1, keepdims=True)


def share_kernel(weights_ref, second_ref, turned_ref, early_ref, out_ref):
    order = second_ref.shape[1] // 2
    left_real, left_imag = second_ref[:, :order].astype(F32), second_ref[:, order:].astype(F32)
    right_real, right_imag = turned_ref[:, :order].astype(F32), turned_ref[:, order:].astype(F32)
    real_part = whole_sum(left_real * right_real - left_imag * right_imag)
    imag_part = whole_sum(left_real * right_imag + left_imag * right_real)
    traces = early_ref[0:1, :] + at_lanes((1, 128), [(4, real_part), (5, imag_part)])
    values = jnp.sum(traces * weights_ref[0:2, :], axis=1, keepdims=True)
    out_ref[...] = values * weights_ref[2:3, : out_ref.shape[1]]


def third_kernel(second_ref, first_ref, chain_ref):
    order = second_ref.shape[1] // 2
    real_part, imag_part = times_rows(second_ref[...], first_ref[...])
    scale = math.sqrt(order)
    chain_ref[:, :order] = (real_part * scale).astype(BF16)
    chain_ref[:, order:] = (imag_part * scale).astype(BF16)


def on_device(
    eigenvectors, gauge_links, perambulators, source_times, insert_offsets, derivative_dirs
):
    spaces, spins, slots = lax.axis_size("space"), lax.axis_size("spin"), lax.axis_size("tm")
    planes, side, modes = eigenvectors.shape[3], eigenvectors.shape[4], eigenvectors.shape[6]
    cells = planes * side * side
    own_rows = perambulators[0]
    count, width = own_rows.shape
    order = width // 2

    field = eigenvectors.reshape((6 * cells, modes))
    fields = [field] + [from_offset(field, "space", step) for step in range(1, spaces)]
    link = jnp.swapaxes(gauge_links.reshape((54, planes, side * side)), 1, 2)
    link = vmem_call(
        links_kernel,
        jax.ShapeDtypeStruct((cells, modes), BF16),
        [pltpu.VMEM(link.shape, F32), pltpu.VMEM((cells, modes), F32)],
        10**9,
    )(link)
    links = [link] + [from_offset(link, "space", step) for step in range(1, spaces)]
    fields[0], own_slab = vmem_call(
        functools.partial(slab_kernel, side),
        (
            jax.ShapeDtypeStruct(field.shape, BF16),
            jax.ShapeDtypeStruct((18 * cells, modes), BF16),
        ),
        [],
        10**6,
    )(field, link)

    held_rows, own_slab = lax.optimization_barrier((own_rows, own_slab))
    far_rows = [from_offset(held_rows, "space", step) for step in range(1, spaces)]

    norm_scale = 1.0 / math.sqrt(6.0 * 4.0 * planes * spaces * side * side)
    rows_shape = jax.ShapeDtypeStruct((count, width), BF16)
    trace_shape = jax.ShapeDtypeStruct((8, 128), F32)
    elements = vmem_call(
        functools.partial(elementals_kernel, side, norm_scale, spaces),
        jax.ShapeDtypeStruct((3, 2, modes, modes), F32),
        [pltpu.VMEM((6 * cells * spaces, 6 * modes), BF16)],
        10**10,
    )(own_slab, *fields, *links)
    wide_shape = jax.ShapeDtypeStruct((count, width), F32)
    operator, own_first, own_wide = vmem_call(
        operator_kernel,
        (jax.ShapeDtypeStruct((4 * modes, 4 * modes), BF16), rows_shape, wide_shape),
        [],
        10**8,
        smem=(0,),
    )(derivative_dirs, elements, own_rows)

    next_first = from_offset(own_first, "tm", 1)

    far_rows, held_first = lax.optimization_barrier((far_rows, own_first))
    piece_shape = jax.ShapeDtypeStruct((count // PIECES, width), BF16)
    far_first = vmem_call(first_kernel, (piece_shape,) * (PIECES * len(far_rows)), [], 10**6)(
        operator, *far_rows
    )
    blocks = [own_first] + [from_offset(held_first, "spin", step) for step in range(1, spins)]
    for at in range(0, len(far_first), PIECES):
        pieces = list(far_first[at : at + PIECES])
        blocks += pieces
        for step in range(1, spins):
            blocks += [from_offset(piece, "spin", step) for piece in pieces]
    first, second, second_wide = vmem_call(
        functools.partial(second_kernel, spaces, spins),
        (jax.ShapeDtypeStruct((order, width), BF16), rows_shape, wide_shape),
        [],
        3 * 10**8,
    )(next_first, *blocks)
    next_second = from_offset(second, "tm", 1)

    turned, weights, elementals, early = vmem_call(
        functools.partial(turn_kernel, spaces, spins),
        (
            rows_shape,
            trace_shape,
            jax.ShapeDtypeStruct((modes // spaces, 3, 2, modes // spins), F32),
            trace_shape,
        ),
        [pltpu.VMEM((max(count, 128), width), F32)],
        10**6,
        smem=(0,),
    )(insert_offsets, source_times[None, :], first, elements, own_wide, second_wide)
    shares = vmem_call(
        share_kernel,
        jax.ShapeDtypeStruct((2, source_times.shape[0]), F32),
        [],
        10**6,
    )(weights, next_second, turned, early)
    chain = vmem_call(third_kernel, rows_shape, [], 10**8)(next_second, first)

    devices = slots * spaces * spins
    if devices & (devices - 1):
        shares = lax.psum(shares, ("tm", "space", "spin"))
    else:
        bits = [1 << at for at in range(devices.bit_length() - 1)]
        while bits:
            low, high = bits[0], bits[-1]
            bits = bits[1:-1]
            masks = [low] if low == high else [low, high, low | high]
            parts = [swapped(shares, devices, mask) for mask in masks]
            shares = functools.reduce(lambda x, y: x + y, parts, shares)
    return (elementals[None], chain[None], shares.T)


def solution(mesh):
    in_specs = (
        P(("cfg", "tm"), None, None, "space", None, None, None),
        P(("cfg", "tm"), None, None, None, None, "space", None),
        P(("cfg", "tm"), ("space", "spin"), None),
        P(),
        P(),
        P(),
    )
    out_specs = (
        P(("cfg", "tm"), "space", None, None, "spin"),
        P(("cfg", "tm"), ("space", "spin"), None),
        P("cfg", None),
    )
    return jax.shard_map(
        on_device, mesh=mesh, in_specs=in_specs, out_specs=out_specs, check_vma=False
    )
```
